32 devices in a mesh: fsdp: 16 (over z, y, x), seq: 2 (over core).
Axes of the slice: x: 2, y: 2, z: 4, core: 2. Of those that a mesh axis runs over, the one named last changes fastest.
Arguments:
- tokens: bfloat16 [32, 1024, 1152], P('fsdp', 'seq'), may hold values from -6 to 6
- timestep: bfloat16 [32, 6912], P('fsdp'), may hold values from -1.5 to 1.5
- text: bfloat16 [32, 120, 1152], P('fsdp', 'seq'), may hold values from -6 to 6
- cotangent: bfloat16 [32, 1024, 1152], P('fsdp', 'seq'), may hold values from -6 to 6
- vectors: bfloat16 [1152, 17], P('fsdp'), may hold values from -1.5 to 1.5
- w_qkv: bfloat16 [1152, 3456], P('fsdp', 'seq'), may hold values from -0.1875 to 0.1875
- w_out: bfloat16 [1152, 1152], P('fsdp', 'seq'), may hold values from -0.5 to 0.5
- w_query2: bfloat16 [1152, 1152], P('fsdp', 'seq'), may hold values from -0.1875 to 0.1875
- w_kv2: bfloat16 [1152, 2304], P('fsdp', 'seq'), may hold values from -0.1875 to 0.1875
- w_out2: bfloat16 [1152, 1152], P('fsdp', 'seq'), may hold values from -0.375 to 0.375
- w_fc1: bfloat16 [1152, 4608], P('fsdp', 'seq'), may hold values from -0.1875 to 0.1875
- w_fc2: bfloat16 [4608, 1152], P('fsdp', 'seq'), may hold values from -0.125 to 0.125
Outputs:
- result: bfloat16 [32, 1024, 1152], P('fsdp', 'seq')
- grad_tokens: float32 [32, 1024, 1152], P('fsdp', 'seq')
- grad_timestep: float32 [32, 6912], P('fsdp')
- grad_text: float32 [32, 120, 1152], P('fsdp', 'seq')
- grad_vectors: float32 [1152, 17], P('fsdp')
- grad_qkv: float32 [1152, 3456], P('fsdp', 'seq')
- grad_out: float32 [1152, 1152], P('fsdp', 'seq')
- grad_query2: float32 [1152, 1152], P('fsdp', 'seq')
- grad_kv2: float32 [1152, 2304], P('fsdp', 'seq')
- grad_out2: float32 [1152, 1152], P('fsdp', 'seq')
- grad_fc1: float32 [1152, 4608], P('fsdp', 'seq')
- grad_fc2: float32 [4608, 1152], P('fsdp', 'seq')
The draws below stay inside these ranges and needn't reach their ends.
All inputs are finite; a program needn't handle non-finite values.
Results may differ from the reference program's by a relative error of at most 0.015.
Values may be sent and summed in bfloat16 or wider, within the bound.
No kernel may reach another device: no remote copies, remote signals or barrier semaphores. Data moves between devices by JAX's collectives and lax.ppermute only.
A program may use at most 512 MiB of HBM per device.

```python
import jax
import jax.numpy as jnp
from jax import lax

D = 1152
HEADS = 16
HEAD_DIM = 72
FF = 4608
TXT = 120
LENGTH = 1024
VECS = 17
IMAGES = 32


def block_levels(rng, shape, split, smallest, high):
    def one(position, shards_of):
        draws = jax.random.uniform(jax.random.fold_in(jax.random.fold_in(rng, 6), position), (shards_of,), jnp.float32, smallest / len(split), high / len(split))
        return jnp.repeat(jnp.exp(draws), shape[position] // shards_of).reshape((-1,) + (1,) * (len(shape) - position - 1))

    gain = one(*split[0])
    for cut in split[1:]:
        gain = gain * one(*cut)
    return gain


def normal_values(stream_key, shape, scale, most, split=(), kind=jnp.bfloat16):
    drawn = scale * jax.random.normal(stream_key, shape, jnp.float32)
    if split:
        drawn = drawn * block_levels(stream_key, shape, split, -0.22, 0.18)
    return jnp.clip(drawn, -most, most).astype(kind)


def setup_inputs(seed: int = 0) -> dict:
    streams_of = jax.random.split(jax.random.key(seed), 13)
    tokens = normal_values(streams_of[0], (IMAGES, LENGTH, D), 1.0, 6.0, ((0, 16), (1, 2)))
    timestep = normal_values(streams_of[1], (IMAGES, 6 * D), 0.3, 1.5, ((0, 16),))
    text = normal_values(streams_of[2], (IMAGES, TXT, D), 1.0, 6.0, ((0, 16), (1, 2)))
    cotangent = normal_values(streams_of[3], (IMAGES, LENGTH, D), 1.0, 6.0, ((0, 16), (1, 2)))
    vectors = normal_values(streams_of[4], (D, VECS), 0.3, 1.5, ((0, 16),))
    w_qkv = normal_values(streams_of[5], (D, 3 * D), D ** -0.5, 0.1875, ((0, 16), (1, 2)))
    w_out = normal_values(streams_of[6], (D, D), (D // 8) ** -0.5, 0.5, ((0, 16), (1, 2)))
    w_query2 = normal_values(streams_of[7], (D, D), D ** -0.5, 0.1875, ((0, 16), (1, 2)))
    w_kv2 = normal_values(streams_of[8], (D, 2 * D), D ** -0.5, 0.1875, ((0, 16), (1, 2)))
    w_out2 = normal_values(streams_of[9], (D, D), (D // 4) ** -0.5, 0.375, ((0, 16), (1, 2)))
    w_fc1 = normal_values(streams_of[10], (D, FF), D ** -0.5, 0.1875, ((0, 16), (1, 2)))
    w_fc2 = normal_values(streams_of[11], (FF, D), (FF // 2) ** -0.5, 0.125, ((0, 16), (1, 2)))
    return dict(tokens=tokens, timestep=timestep, text=text, cotangent=cotangent, vectors=vectors, w_qkv=w_qkv, w_out=w_out, w_query2=w_query2, w_kv2=w_kv2, w_out2=w_out2, w_fc1=w_fc1, w_fc2=w_fc2)


@jax.custom_vjp
def low(v):
    return lax.optimization_barrier(v.astype(jnp.bfloat16)).astype(jnp.float32)

@jax.custom_vjp
def low_back(v):
    return v

def low_keep(v):
    return (low(v), None)

def low_pass(kept, grad):
    return (grad,)

def back_keep(v):
    return (v, None)

def back_low(kept, grad):
    return (low(grad),)
low.defvjp(low_keep, low_pass)
low_back.defvjp(back_keep, back_low)
norm_eps = 1e-06
gelu_root = 0.7978845608028654
gelu_cube = 0.044715

def norm_rows(inputs):
    center = inputs - lax.optimization_barrier(jnp.mean(inputs, axis=-1, keepdims=True))
    spread = lax.optimization_barrier(jnp.mean(center * center, axis=-1, keepdims=True))
    return center * lax.rsqrt(spread + norm_eps)

def gelu_tanh(inputs):
    return 0.5 * inputs * (1.0 + jnp.tanh(gelu_root * (inputs + gelu_cube * inputs * inputs * inputs)))

def matmul(left_side, right_side):
    return jnp.dot(left_side, right_side, precision=lax.Precision.HIGHEST)

def attention(queries, key_rows, value_rows):
    row_count = queries.shape[0]
    q_heads = queries.reshape(row_count, HEADS, HEAD_DIM)
    k_heads = key_rows.reshape(key_rows.shape[0], HEADS, HEAD_DIM)
    v_heads = value_rows.reshape(value_rows.shape[0], HEADS, HEAD_DIM)
    scores = low_back(jnp.einsum('qhd,khd->hqk', q_heads, k_heads, precision=lax.Precision.HIGHEST) * HEAD_DIM ** (-0.5))
    row_top = lax.optimization_barrier(jnp.max(scores, axis=-1, keepdims=True))
    exponent = jnp.exp(scores - row_top)
    attn_weights = low(exponent / lax.optimization_barrier(jnp.sum(exponent, axis=-1, keepdims=True)))
    mixed = jnp.einsum('hqk,khd->qhd', attn_weights, v_heads, precision=lax.Precision.HIGHEST)
    return mixed.reshape(row_count, D)

def image_layer(inputs, time_row, text_rows, vectors, w_qkv, w_out, w_query2, w_kv2, w_out2, w_fc1, w_fc2):
    modulation = vectors[:, :6].T + time_row.reshape(6, D)
    zero_bias = jnp.zeros_like(vectors[:, 0])
    h_attn = low(norm_rows(inputs) * (1.0 + modulation[1]) + modulation[0])
    qkv_bias = jnp.concatenate([vectors[:, 6], zero_bias, vectors[:, 7]])
    qkv_rows = low(low_back(matmul(h_attn, w_qkv) + qkv_bias))
    attn_low = low(low_back(attention(qkv_rows[:, :D], qkv_rows[:, D:2 * D], qkv_rows[:, 2 * D:])))
    attn_proj = low_back(matmul(attn_low, w_out) + vectors[:, 8])
    after_attn = inputs + modulation[2] * attn_proj
    cross_query = low(low_back(matmul(low(after_attn), w_query2) + vectors[:, 9]))
    kv_bias = jnp.concatenate([zero_bias, vectors[:, 10]])
    text_kv = low(low_back(matmul(text_rows, w_kv2) + kv_bias))
    cross_low = low(low_back(attention(cross_query, text_kv[:, :D], text_kv[:, D:])))
    after_cross = after_attn + low_back(matmul(cross_low, w_out2) + vectors[:, 11])
    h_mlp = low(norm_rows(after_cross) * (1.0 + modulation[4]) + modulation[3])
    hidden_pre = low_back(matmul(h_mlp, w_fc1) + vectors[:, 13:].T.reshape(FF))
    hidden_low = low(gelu_tanh(hidden_pre))
    mlp_out = low_back(matmul(hidden_low, w_fc2) + vectors[:, 12])
    return after_cross + modulation[5] * mlp_out

def reference(tokens, timestep, text, cotangent, vectors, w_qkv, w_out, w_query2, w_kv2, w_out2, w_fc1, w_fc2):

    def forward(tok_f, time_f, text_f, vec_f, qkv_f, out_f, query_f, kv_f, out2_f, fc1_f, fc2_f):
        layer_fn = jax.checkpoint(image_layer)

        def one_image(element):
            return layer_fn(element[0], element[1], element[2], vec_f, qkv_f, out_f, query_f, kv_f, out2_f, fc1_f, fc2_f)
        return lax.map(one_image, (tok_f, time_f, text_f))
    floats = tuple((operand.astype(jnp.float32) for operand in (tokens, timestep, text, vectors, w_qkv, w_out, w_query2, w_kv2, w_out2, w_fc1, w_fc2)))
    output, pullback = jax.vjp(forward, *floats)
    gradients = pullback(cotangent.astype(output.dtype))
    return (output.astype(jnp.bfloat16), gradients[0], gradients[1], gradients[2], gradients[3], gradients[4], gradients[5], gradients[6], gradients[7], gradients[8], gradients[9], gradients[10])
```

```python
import functools

import jax
import jax.numpy as jnp
from jax import lax
from jax.experimental import pallas as pl
from jax.experimental.pallas import tpu as pltpu
from jax.sharding import PartitionSpec as P

D = 1152
HEADS = 16
HEAD_DIM = 72
MEBI = 1024 * 1024
VMEM_LIMIT = 56 * MEBI
COST_SHARE = 1000

norm_eps = 1e-06
gelu_root = 0.7978845608028654
gelu_cube = 0.044715


def norm_rows(inputs):
    center = inputs - jnp.mean(inputs, axis=-1, keepdims=True)
    spread = jnp.mean(center * center, axis=-1, keepdims=True)
    return center * lax.rsqrt(spread + norm_eps)


def gelu_tanh(inputs):
    return (
        0.5 * inputs * (1.0 + jnp.tanh(gelu_root * (inputs + gelu_cube * inputs * inputs * inputs)))
    )


def modulated(inputs, shift_rows, scale_rows):
    return norm_rows(inputs) * (1.0 + scale_rows) + shift_rows


def flatten(tensor):
    return tensor.reshape(-1, tensor.shape[-1])


def low(values):
    return values.astype(jnp.bfloat16)


def dot_nt(left, right):
    return lax.dot_general(left, right, (((1,), (1,)), ((), ())), preferred_element_type=jnp.float32)


def dot_tn(left, right):
    return lax.dot_general(left, right, (((0,), (0,)), ((), ())), preferred_element_type=jnp.float32)


def cost(flops, bytes_accessed, transcendentals):
    return pl.CostEstimate(
        flops=flops // COST_SHARE,
        bytes_accessed=bytes_accessed // COST_SHARE,
        transcendentals=transcendentals // COST_SHARE,
    )


LANES = 256
LOG2E = 1.4426950408889634
SCALE = HEAD_DIM**-0.5


def contract_last(left, right):
    return lax.dot_general(left, right, (((1,), (1,)), ((), ())), preferred_element_type=jnp.float32)


def matmul(left, right):
    return jnp.dot(left, right, preferred_element_type=jnp.float32)


def head_window(head):
    first = head * HEAD_DIM
    start = pl.multiple_of(jnp.minimum(first // 128 * 128, D - LANES), 128)
    column = start + lax.broadcasted_iota(jnp.int32, (1, LANES), 1)
    inside = (column >= first) & (column < first + HEAD_DIM)
    return pl.ds(start, LANES), inside


def fill_transposed(rows_ref, columns_scr):
    columns_scr[...] = jnp.transpose(rows_ref[0].astype(jnp.float32)).astype(jnp.bfloat16)


def aligned_rows(pair, odd):
    return pl.ds(pl.multiple_of(pair * 144 + 64 * odd, 16), 80)


def head_rows(head):
    return pl.ds(pl.multiple_of(head * HEAD_DIM, 8), HEAD_DIM)


def for_heads(ahead, then):
    ahead(0, 0)

    def two_heads(pair, carry):
        ahead(2 * pair + 1, 1)
        then(2 * pair, pair, 0)
        ahead(jnp.minimum(2 * pair + 2, HEADS - 1), 0)
        then(2 * pair + 1, pair, 1)
        return carry

    lax.fori_loop(0, HEADS // 2, two_heads, 0)


def attend_forward_kernel(q_ref, k_ref, v_ref, o_ref, lse_ref, vt_scr, ot_scr, s_scr):
    @pl.when(pl.program_id(1) == 0)
    def _():
        fill_transposed(v_ref, vt_scr)

    def ahead(head, slot):
        window, inside = head_window(head)
        q_head = q_ref[0, :, window] * inside.astype(jnp.bfloat16)
        s_scr[slot] = contract_last(k_ref[0, :, window], q_head)

    def then(head, pair, slot):
        scores = s_scr[slot]
        top = jnp.max(scores, axis=0, keepdims=True)
        weights = jnp.exp2((scores - top) * (SCALE * LOG2E))
        total = jnp.sum(weights, axis=0, keepdims=True)
        mixed = matmul(vt_scr[aligned_rows(pair, slot), :], weights.astype(jnp.bfloat16))
        ot_scr[head_rows(head), :] = mixed[8 * slot : 8 * slot + HEAD_DIM] * (1.0 / total)
        lse_ref[0, pl.ds(head, 1), :] = top * (SCALE * LOG2E) + jnp.log2(total)

    for_heads(ahead, then)
    o_ref[0] = jnp.transpose(ot_scr[...]).astype(jnp.bfloat16)


def attend_forward(queries, keys, values, row_block):
    (q_arr, q_blk), (k_arr, k_blk), (v_arr, v_blk) = queries, keys, values
    batch, rows, key_rows = q_arr.shape[0], q_arr.shape[1], k_arr.shape[1]
    block = min(row_block, rows)
    return pl.pallas_call(
        attend_forward_kernel,
        grid=(batch, rows // block),
        in_specs=[
            pl.BlockSpec((1, block, D), lambda b, i: (b, i, q_blk)),
            pl.BlockSpec((1, key_rows, D), lambda b, i: (b, 0, k_blk)),
            pl.BlockSpec((1, key_rows, D), lambda b, i: (b, 0, v_blk)),
        ],
        out_specs=[
            pl.BlockSpec((1, block, D), lambda b, i: (b, i, 0)),
            pl.BlockSpec((1, HEADS, block), lambda b, i: (b, 0, i)),
        ],
        out_shape=[
            jax.ShapeDtypeStruct((batch, rows, D), jnp.bfloat16),
            jax.ShapeDtypeStruct((batch, HEADS, rows), jnp.float32),
        ],
        scratch_shapes=[
            pltpu.VMEM((D, key_rows), jnp.bfloat16),
            pltpu.VMEM((D, block), jnp.float32),
            pltpu.VMEM((2, key_rows, block), jnp.float32),
        ],
        compiler_params=pltpu.CompilerParams(vmem_limit_bytes=48 * MEBI),
        cost_estimate=cost(
            flops=4 * batch * rows * key_rows * HEADS * LANES,
            bytes_accessed=4 * batch * (rows + key_rows) * D,
            transcendentals=batch * rows * key_rows * HEADS,
        ),
    )(q_arr, k_arr, v_arr)


def attend_backward_kernel(
    fused, q_ref, k_ref, v_ref, g_ref, o_ref, lse_ref, *rest
):
    if fused:
        out_ref, kt_scr, dk_scr, dv_scr, dqt_scr, dot_scr, s_scr, g_scr = rest
    else:
        dq_ref, dkv_ref, kt_scr, dk_scr, dv_scr, dqt_scr, dot_scr, s_scr, g_scr = rest
    step = pl.program_id(1)
    block = q_ref.shape[1]

    @pl.when(step == 0)
    def _():
        fill_transposed(k_ref, kt_scr)
        dk_scr[...] = jnp.zeros_like(dk_scr)
        dv_scr[...] = jnp.zeros_like(dv_scr)

    products = g_ref[0].astype(jnp.float32) * o_ref[0].astype(jnp.float32)
    head_row = lax.broadcasted_iota(jnp.int32, (HEADS, D), 0) * HEAD_DIM
    column = lax.broadcasted_iota(jnp.int32, (HEADS, D), 1)
    member = ((column >= head_row) & (column < head_row + HEAD_DIM)).astype(jnp.bfloat16)
    high = products.astype(jnp.bfloat16)
    rest_low = (products - high.astype(jnp.float32)).astype(jnp.bfloat16)
    dot_scr[...] = contract_last(member, high) + contract_last(member, rest_low)

    def masked(ref, head):
        window, inside = head_window(head)
        return ref[0, :, window] * inside.astype(jnp.bfloat16)

    def ahead(head, slot):
        window, _ = head_window(head)
        s_scr[slot] = contract_last(k_ref[0, :, window], masked(q_ref, head))
        g_scr[slot] = contract_last(v_ref[0, :, window], masked(g_ref, head))

    def then(head, pair, slot):
        window, _ = head_window(head)
        row = pl.ds(head, 1)
        weights = jnp.exp2(s_scr[slot] * (SCALE * LOG2E) - lse_ref[0, row, :])
        grad_scores = (weights * (g_scr[slot] - dot_scr[row, :])).astype(jnp.bfloat16)
        dv_scr[:, window] += matmul(weights.astype(jnp.bfloat16), masked(g_ref, head))
        dk_scr[:, window] += matmul(grad_scores, masked(q_ref, head))
        dq_rows = matmul(kt_scr[aligned_rows(pair, slot), :], grad_scores)
        dqt_scr[head_rows(head), :] = dq_rows[8 * slot : 8 * slot + HEAD_DIM]

    for_heads(ahead, then)
    grad_q = (jnp.transpose(dqt_scr[...]) * SCALE).astype(jnp.bfloat16)
    if fused:
        out_ref[0, pl.ds(pl.multiple_of(step * block, block), block), :D] = grad_q
    else:
        dq_ref[0] = grad_q

    @pl.when(step == pl.num_programs(1) - 1)
    def _():
        if fused:
            out_ref[0, :, D : 2 * D] = (dk_scr[...] * SCALE).astype(out_ref.dtype)
            out_ref[0, :, 2 * D :] = dv_scr[...].astype(out_ref.dtype)
        else:
            dkv_ref[0, :, :D] = (dk_scr[...] * SCALE).astype(dkv_ref.dtype)
            dkv_ref[0, :, D:] = dv_scr[...].astype(dkv_ref.dtype)


def attend_backward(queries, keys, values, grad_mixed, mixed, lse, row_block, fused, kv_dtype):
    (q_arr, q_blk), (k_arr, k_blk), (v_arr, v_blk) = queries, keys, values
    batch, rows, key_rows = q_arr.shape[0], q_arr.shape[1], k_arr.shape[1]
    block = min(row_block, rows)
    if fused:
        out_specs = [pl.BlockSpec((1, key_rows, 3 * D), lambda b, i: (b, 0, 0))]
        out_shape = [jax.ShapeDtypeStruct((batch, key_rows, 3 * D), jnp.bfloat16)]
    else:
        out_specs = [
            pl.BlockSpec((1, block, D), lambda b, i: (b, i, 0)),
            pl.BlockSpec((1, key_rows, 2 * D), lambda b, i: (b, 0, 0)),
        ]
        out_shape = [
            jax.ShapeDtypeStruct((batch, rows, D), jnp.bfloat16),
            jax.ShapeDtypeStruct((batch, key_rows, 2 * D), kv_dtype),
        ]
    return pl.pallas_call(
        functools.partial(attend_backward_kernel, fused),
        grid=(batch, rows // block),
        in_specs=[
            pl.BlockSpec((1, block, D), lambda b, i: (b, i, q_blk)),
            pl.BlockSpec((1, key_rows, D), lambda b, i: (b, 0, k_blk)),
            pl.BlockSpec((1, key_rows, D), lambda b, i: (b, 0, v_blk)),
            pl.BlockSpec((1, block, D), lambda b, i: (b, i, 0)),
            pl.BlockSpec((1, block, D), lambda b, i: (b, i, 0)),
            pl.BlockSpec((1, HEADS, block), lambda b, i: (b, 0, i)),
        ],
        out_specs=out_specs,
        out_shape=out_shape,
        scratch_shapes=[
            pltpu.VMEM((D, key_rows), jnp.bfloat16),
            pltpu.VMEM((key_rows, D), jnp.float32),
            pltpu.VMEM((key_rows, D), jnp.float32),
            pltpu.VMEM((D, block), jnp.float32),
            pltpu.VMEM((HEADS, block), jnp.float32),
            pltpu.VMEM((2, key_rows, block), jnp.float32),
            pltpu.VMEM((2, key_rows, block), jnp.float32),
        ],
        compiler_params=pltpu.CompilerParams(vmem_limit_bytes=VMEM_LIMIT),
        cost_estimate=cost(
            flops=10 * batch * rows * key_rows * HEADS * LANES,
            bytes_accessed=2 * batch * (3 * rows + 2 * key_rows + 3 * key_rows) * D,
            transcendentals=batch * rows * key_rows * HEADS,
        ),
    )(q_arr, k_arr, v_arr, grad_mixed, mixed, lse)


MLP_TILE = 768


def row_chunks(rows, most=256):
    size = min(most, rows)
    return [slice(first, first + size) for first in range(0, rows, size)]


def lagged(rows, product, use, most=256):
    waiting = None
    for part in row_chunks(rows, most):
        value = product(part)
        if waiting is not None:
            use(*waiting)
        waiting = (part, value)
    use(*waiting)


def mlp_first_kernel(h_ref, w_ref, b_ref, low_ref, slope_ref):
    def product(part):
        return matmul(h_ref[0, part], w_ref[...])

    def use(part, value):
        value = value + b_ref[...]
        square = value * value
        bent = jnp.tanh(value * (gelu_root * gelu_cube * square + gelu_root))
        half = 0.5 * value
        low_ref[0, part] = low(half * bent + half)
        inner = 3.0 * gelu_root * gelu_cube * square + gelu_root
        slope_ref[0, part] = low(half * inner * (1.0 - bent * bent) + (0.5 * bent + 0.5))

    lagged(h_ref.shape[1], product, use)


def mlp_first(h_mlp, whole, bias):
    batch, rows = h_mlp.shape[:2]
    tile = pl.BlockSpec((1, rows, MLP_TILE), lambda b, i: (b, 0, i))
    shape = jax.ShapeDtypeStruct((batch, rows, 2 * D), jnp.bfloat16)
    return pl.pallas_call(
        mlp_first_kernel,
        grid=(batch, 2 * D // MLP_TILE),
        in_specs=[
            pl.BlockSpec((1, rows, D), lambda b, i: (b, 0, 0)),
            pl.BlockSpec((D, MLP_TILE), lambda b, i: (0, i)),
            pl.BlockSpec((1, MLP_TILE), lambda b, i: (0, i)),
        ],
        out_specs=[tile, tile],
        out_shape=[shape, shape],
        compiler_params=pltpu.CompilerParams(vmem_limit_bytes=VMEM_LIMIT),
        cost_estimate=cost(
            flops=4 * batch * rows * D * D,
            bytes_accessed=2 * (batch * rows * 5 * D + 2 * D * D),
            transcendentals=2 * batch * rows * D,
        ),
    )(h_mlp, whole, bias)


def mlp_second_kernel(
    lo_ref, lc_ref, wo_ref, wc_ref, b_ref, x_ref, gate_ref, e_ref,
    out_ref, gm_ref, gate_sum_ref, gm_sum_ref, acc_scr,
):
    step = pl.program_id(1)

    @pl.when(step == 0)
    def _():
        acc_scr[...] = matmul(lo_ref[0], wo_ref[...])

    @pl.when(step == 1)
    def _():
        acc_scr[...] += matmul(lo_ref[0], wo_ref[...])

    @pl.when(step == 2)
    def _():
        acc_scr[...] += matmul(lc_ref[0], wc_ref[...])

    @pl.when(step == 3)
    def _():
        gate = gate_ref[0]
        sums = [0.0, 0.0]

        def product(part):
            return acc_scr[part] + matmul(lc_ref[0, part], wc_ref[...])

        def use(part, value):
            mlp_out = value + b_ref[...]
            grad = e_ref[0, part].astype(jnp.float32)
            out_ref[0, part] = low(x_ref[0, part] + gate * mlp_out)
            grad_mlp = low(gate * grad)
            gm_ref[0, part] = grad_mlp
            sums[0] += jnp.sum(grad * mlp_out, axis=0, keepdims=True)
            sums[1] += jnp.sum(grad_mlp.astype(jnp.float32), axis=0, keepdims=True)

        lagged(lo_ref.shape[1], product, use)
        gate_sum_ref[0], gm_sum_ref[0] = sums


def mlp_second(lows, wholes, bias, after_cross, gate, cotangent):
    batch, rows = after_cross.shape[:2]
    full = pl.BlockSpec((1, rows, D), lambda b, k: (b, 0, 0))
    row = pl.BlockSpec((1, 1, D), lambda b, k: (b, 0, 0))

    def first(k):
        return jnp.minimum(k, 1)

    def later(k):
        return jnp.maximum(k - 2, 0)

    return pl.pallas_call(
        mlp_second_kernel,
        grid=(batch, 4),
        in_specs=[
            pl.BlockSpec((1, rows, D), lambda b, k: (b, 0, first(k))),
            pl.BlockSpec((1, rows, D), lambda b, k: (b, 0, later(k))),
            pl.BlockSpec((D, D), lambda b, k: (0, 2 + first(k))),
            pl.BlockSpec((D, D), lambda b, k: (0, 2 + later(k))),
            pl.BlockSpec((1, D), lambda b, k: (0, 0)),
            full,
            row,
            full,
        ],
        out_specs=[full, full, row, row],
        out_shape=[
            jax.ShapeDtypeStruct((batch, rows, D), jnp.bfloat16),
            jax.ShapeDtypeStruct((batch, rows, D), jnp.bfloat16),
            jax.ShapeDtypeStruct((batch, 1, D), jnp.float32),
            jax.ShapeDtypeStruct((batch, 1, D), jnp.float32),
        ],
        scratch_shapes=[pltpu.VMEM((rows, D), jnp.float32)],
        compiler_params=pltpu.CompilerParams(vmem_limit_bytes=56 * MEBI),
        cost_estimate=cost(
            flops=8 * batch * rows * D * D,
            bytes_accessed=batch * rows * D * 18 + 8 * D * D,
            transcendentals=0,
        ),
    )(*lows, *wholes, bias, after_cross, gate, cotangent)


def mlp_slope_kernel(g_ref, w_ref, slope_ref, gp_ref, sum_ref):
    sums = [0.0]

    def product(part):
        return contract_last(g_ref[0, part], w_ref[...])

    def use(part, value):
        grad = low(value * slope_ref[0, part].astype(jnp.float32))
        gp_ref[0, part] = grad
        sums[0] += jnp.sum(grad.astype(jnp.float32), axis=0, keepdims=True)

    lagged(g_ref.shape[1], product, use)
    sum_ref[0] = sums[0]


def mlp_slope(grad_mlp, whole, slope):
    batch, rows = grad_mlp.shape[:2]
    return pl.pallas_call(
        mlp_slope_kernel,
        grid=(batch, 2),
        in_specs=[
            pl.BlockSpec((1, rows, D), lambda b, i: (b, 0, 0)),
            pl.BlockSpec((D, D), lambda b, i: (0, 2 + i)),
            pl.BlockSpec((1, rows, D), lambda b, i: (b, 0, i)),
        ],
        out_specs=[
            pl.BlockSpec((1, rows, D), lambda b, i: (b, 0, i)),
            pl.BlockSpec((1, 1, D), lambda b, i: (b, 0, i)),
        ],
        out_shape=[
            jax.ShapeDtypeStruct((batch, rows, 2 * D), jnp.bfloat16),
            jax.ShapeDtypeStruct((batch, 1, 2 * D), jnp.float32),
        ],
        compiler_params=pltpu.CompilerParams(vmem_limit_bytes=42 * MEBI),
        cost_estimate=cost(
            flops=4 * batch * rows * D * D,
            bytes_accessed=2 * (batch * rows * 5 * D + 2 * D * D),
            transcendentals=0,
        ),
    )(grad_mlp, whole, slope)


def norm_backward(inputs, grad, scale_rows):
    center = inputs - jnp.mean(inputs, axis=-1, keepdims=True)
    spread = jnp.mean(center * center, axis=-1, keepdims=True)
    root = lax.rsqrt(spread + norm_eps)
    normed = center * root
    grad_shift = jnp.sum(grad, axis=0, keepdims=True)
    grad_scale = jnp.sum(grad * normed, axis=0, keepdims=True)
    inner = grad * (1.0 + scale_rows)
    along = jnp.mean(inner * normed, axis=-1, keepdims=True)
    inner = root * (inner - jnp.mean(inner, axis=-1, keepdims=True) - normed * along)
    return inner, grad_shift, grad_scale


def mlp_input_kernel(
    go_ref, gc_ref, wo_ref, wc_ref, x_ref, scale_ref, e_ref,
    gx_ref, gl_ref, shift_sum_ref, scale_sum_ref, gl_sum_ref, acc_scr,
):
    step = pl.program_id(1)

    @pl.when(step == 0)
    def _():
        acc_scr[...] = jnp.zeros_like(acc_scr)

    @pl.when(step < 3)
    def _():
        acc_scr[...] += contract_last(go_ref[0], wo_ref[...])

    @pl.when((step >= 3) & (step < 5))
    def _():
        acc_scr[...] += contract_last(gc_ref[0], wc_ref[...])

    @pl.when(step == 5)
    def _():
        sums = [0.0, 0.0, 0.0]

        def product(part):
            return acc_scr[part] + contract_last(gc_ref[0, part], wc_ref[...])

        def use(part, grad):
            inner, grad_shift, grad_scale = norm_backward(x_ref[0, part], grad, scale_ref[0])
            inner += e_ref[0, part].astype(jnp.float32)
            gx_ref[0, part] = inner
            gl_ref[0, part] = low(inner)
            low_sum = jnp.sum(low(inner).astype(jnp.float32), axis=0, keepdims=True)
            for at, new in enumerate((grad_shift, grad_scale, low_sum)):
                sums[at] += new

        lagged(go_ref.shape[1], product, use)
        shift_sum_ref[0], scale_sum_ref[0], gl_sum_ref[0] = sums


def mlp_input(grads, wholes, after_cross, scale_rows, cotangent):
    batch, rows = after_cross.shape[:2]
    full = pl.BlockSpec((1, rows, D), lambda b, k: (b, 0, 0))
    row = pl.BlockSpec((1, 1, D), lambda b, k: (b, 0, 0))
    row_shape = jax.ShapeDtypeStruct((batch, 1, D), jnp.float32)

    def first(k):
        return jnp.minimum(k, 2)

    def later(k):
        return jnp.maximum(k - 3, 0)

    return pl.pallas_call(
        mlp_input_kernel,
        grid=(batch, 6),
        in_specs=[
            pl.BlockSpec((1, rows, MLP_TILE), lambda b, k: (b, 0, first(k))),
            pl.BlockSpec((1, rows, MLP_TILE), lambda b, k: (b, 0, later(k))),
            pl.BlockSpec((D, MLP_TILE), lambda b, k: (0, first(k))),
            pl.BlockSpec((D, MLP_TILE), lambda b, k: (0, later(k))),
            full,
            row,
            full,
        ],
        out_specs=[full, full, row, row, row],
        out_shape=[
            jax.ShapeDtypeStruct((batch, rows, D), jnp.float32),
            jax.ShapeDtypeStruct((batch, rows, D), jnp.bfloat16),
            row_shape,
            row_shape,
            row_shape,
        ],
        scratch_shapes=[pltpu.VMEM((rows, D), jnp.float32)],
        compiler_params=pltpu.CompilerParams(vmem_limit_bytes=56 * MEBI),
        cost_estimate=cost(
            flops=8 * batch * rows * D * D,
            bytes_accessed=batch * rows * D * 20 + 8 * D * D,
            transcendentals=0,
        ),
    )(*grads, *wholes, after_cross, scale_rows, cotangent)


def attend_input_kernel(
    g_ref, w_ref, x_ref, scale_ref, r_ref,
    gx_ref, shift_sum_ref, scale_sum_ref, g_sum_ref, acc_scr,
):
    step = pl.program_id(1)
    g_sum_ref[0] = jnp.sum(g_ref[0].astype(jnp.float32), axis=0, keepdims=True)

    @pl.when(step == 0)
    def _():
        acc_scr[...] = contract_last(g_ref[0], w_ref[...])

    @pl.when(step == 1)
    def _():
        acc_scr[...] += contract_last(g_ref[0], w_ref[...])

    @pl.when(step == 2)
    def _():
        sums = [0.0, 0.0]

        def product(part):
            return acc_scr[part] + contract_last(g_ref[0, part], w_ref[...])

        def use(part, grad):
            inputs = x_ref[0, part].astype(jnp.float32)
            inner, grad_shift, grad_scale = norm_backward(inputs, grad, scale_ref[0])
            gx_ref[0, part] = inner + r_ref[0, part]
            sums[0] += grad_shift
            sums[1] += grad_scale

        lagged(g_ref.shape[1], product, use)
        shift_sum_ref[0], scale_sum_ref[0] = sums


def attend_input(grad_qkv, weight, tokens, scale_rows, grad_attn):
    batch, rows = tokens.shape[:2]
    full = pl.BlockSpec((1, rows, D), lambda b, k: (b, 0, 0))
    row = pl.BlockSpec((1, 1, D), lambda b, k: (b, 0, 0))
    row_shape = jax.ShapeDtypeStruct((batch, 1, D), jnp.float32)
    return pl.pallas_call(
        attend_input_kernel,
        grid=(batch, 3),
        in_specs=[
            pl.BlockSpec((1, rows, D), lambda b, k: (b, 0, k)),
            pl.BlockSpec((D, D), lambda b, k: (0, k)),
            full,
            row,
            full,
        ],
        out_specs=[full, row, row, pl.BlockSpec((1, 1, D), lambda b, k: (b, 0, k))],
        out_shape=[
            jax.ShapeDtypeStruct((batch, rows, D), jnp.float32),
            row_shape,
            row_shape,
            jax.ShapeDtypeStruct((batch, 1, 3 * D), jnp.float32),
        ],
        scratch_shapes=[pltpu.VMEM((rows, D), jnp.float32)],
        compiler_params=pltpu.CompilerParams(vmem_limit_bytes=56 * MEBI),
        cost_estimate=cost(
            flops=6 * batch * rows * D * D,
            bytes_accessed=batch * rows * D * 16 + 6 * D * D,
            transcendentals=0,
        ),
    )(grad_qkv, weight, tokens, scale_rows, grad_attn)


def self_output_kernel(
    m_ref, wo_ref, bo_ref, x_ref, gate_ref, wq_ref, bq_ref, proj_ref, sum_ref, low_ref, query_ref
):
    def product(part):
        proj = matmul(m_ref[0, part], wo_ref[...]) + bo_ref[...]
        proj_ref[0, part] = proj
        after_attn = x_ref[0, part].astype(jnp.float32) + gate_ref[0] * proj
        sum_ref[0, part] = after_attn
        low_ref[0, part] = low(after_attn)
        return low(after_attn)

    def use(part, value):
        query_ref[0, part] = low(matmul(value, wq_ref[...]) + bq_ref[...])

    lagged(m_ref.shape[1], product, use, 128)


def self_output(mixed, w_out, out_bias, tokens, gate, w_query, query_bias):
    batch, rows = mixed.shape[:2]
    block = min(256, rows)
    part = pl.BlockSpec((1, block, D), lambda b, i: (b, i, 0))
    whole = pl.BlockSpec((D, D), lambda b, i: (0, 0))
    row = pl.BlockSpec((1, D), lambda b, i: (0, 0))
    wide = jax.ShapeDtypeStruct((batch, rows, D), jnp.float32)
    narrow = jax.ShapeDtypeStruct((batch, rows, D), jnp.bfloat16)
    return pl.pallas_call(
        self_output_kernel,
        grid=(batch, rows // block),
        in_specs=[
            part,
            whole,
            row,
            part,
            pl.BlockSpec((1, 1, D), lambda b, i: (b, 0, 0)),
            whole,
            row,
        ],
        out_specs=[part] * 4,
        out_shape=[wide, wide, narrow, narrow],
        compiler_params=pltpu.CompilerParams(vmem_limit_bytes=44 * MEBI),
        cost_estimate=cost(
            flops=4 * batch * rows * D * D,
            bytes_accessed=batch * rows * D * 16 + 4 * D * D,
            transcendentals=0,
        ),
    )(mixed, w_out, out_bias, tokens, gate, w_query, query_bias)


def cross_output_kernel(m_ref, w_ref, b_ref, x_ref, shift_ref, scale_ref, sum_ref, h_ref):
    def product(part):
        return matmul(m_ref[0, part], w_ref[...])

    def use(part, value):
        after_cross = x_ref[0, part] + (value + b_ref[...])
        sum_ref[0, part] = after_cross
        h_ref[0, part] = low(modulated(after_cross, shift_ref[0], scale_ref[0]))

    lagged(m_ref.shape[1], product, use, 128)


def cross_output(mixed, weight, bias, after_attn, shift_rows, scale_rows):
    batch, rows = mixed.shape[:2]
    block = min(256, rows)
    part = pl.BlockSpec((1, block, D), lambda b, i: (b, i, 0))
    row = pl.BlockSpec((1, 1, D), lambda b, i: (b, 0, 0))
    return pl.pallas_call(
        cross_output_kernel,
        grid=(batch, rows // block),
        in_specs=[
            part,
            pl.BlockSpec((D, D), lambda b, i: (0, 0)),
            pl.BlockSpec((1, D), lambda b, i: (0, 0)),
            part,
            row,
            row,
        ],
        out_specs=[part, part],
        out_shape=[
            jax.ShapeDtypeStruct((batch, rows, D), jnp.float32),
            jax.ShapeDtypeStruct((batch, rows, D), jnp.bfloat16),
        ],
        compiler_params=pltpu.CompilerParams(vmem_limit_bytes=36 * MEBI),
        cost_estimate=cost(
            flops=2 * batch * rows * D * D,
            bytes_accessed=batch * rows * D * 12 + 2 * D * D,
            transcendentals=0,
        ),
    )(mixed, weight, bias, after_attn, shift_rows, scale_rows)


def chip_flip(count, bit):
    return [(chip, chip ^ bit) for chip in range(count)]


def chip_shift(count, steps):
    return [(chip, (chip + 4 * steps) % count) for chip in range(count)]


def pick(tensor, index, axis):
    return lax.dynamic_index_in_dim(tensor, index, axis, keepdims=False)


def stack_kernel(*refs):
    for at, ref in enumerate(refs[:-1]):
        refs[-1][at] = ref[...]


def column_pieces(shard):
    count = lax.axis_size("fsdp")
    blocks = [shard] + [
        lax.ppermute(shard, "fsdp", chip_shift(count, -step)) for step in range(1, count // 4)
    ]
    return pl.pallas_call(
        stack_kernel,
        out_shape=jax.ShapeDtypeStruct((len(blocks), *shard.shape), shard.dtype),
        compiler_params=pltpu.CompilerParams(vmem_limit_bytes=32 * MEBI),
    )(*blocks)


def near_pieces(column):
    count = lax.axis_size("fsdp")
    return [
        column,
        lax.ppermute(column, "fsdp", chip_flip(count, 2)),
        lax.ppermute(column, "fsdp", chip_flip(count, 1)),
    ]


def far_pieces(near, split):
    count = lax.axis_size("fsdp")
    return [
        lax.ppermute(near[1][..., :split], "fsdp", chip_flip(count, 1)),
        lax.ppermute(near[2][..., split:], "fsdp", chip_flip(count, 2)),
    ]


def piece_columns(refs, start, width):
    blocks = []
    for ref in refs:
        columns = ref.shape[2]
        first, last = max(start, 0), min(start + width, columns)
        if first < last:
            blocks.append(ref[0, :, first:last])
        start -= columns
    return blocks


def assemble_kernel(regions, counts, place, *refs):
    y, x, core = place[1], place[2], place[3]
    sides = []
    for count in counts:
        sides.append(refs[:count])
        refs = refs[count:]

    def write(order):
        for flip_y, flip_x in ((0, 0), (1, 0), (0, 1), (1, 1)):
            chip = (y ^ flip_y) * 2 + (x ^ flip_x)
            near = flip_y + 2 * flip_x
            for out, (start, width) in zip(refs, regions):
                blocks = []
                for side in order:
                    pieces = sides[side][near : near + 1] if near < 3 else sides[side][3:]
                    blocks.extend(piece_columns(pieces, start, width))
                out[0, chip] = blocks[0] if len(blocks) == 1 else jnp.concatenate(blocks, axis=1)

    if len(counts) == 1:
        write((0,))
    else:
        pl.when(core == 0)(lambda: write((0, 1)))
        pl.when(core != 0)(lambda: write((1, 0)))


def assemble(sides, regions):
    count = lax.axis_size("fsdp")
    deep = count // 4
    chip = lax.axis_index("fsdp")
    place = jnp.stack([chip // 4, chip // 2 % 2, chip % 2, lax.axis_index("seq")])
    rows = sides[0][0].shape[1]
    widths = [len(sides) * width for _, width in regions]

    def from_z(i, place):
        return (lax.rem(i - place[0] + deep, deep), 0, 0)

    ins = [piece for side in sides for piece in side]
    outs = pl.pallas_call(
        functools.partial(assemble_kernel, regions, [len(side) for side in sides]),
        grid_spec=pltpu.PrefetchScalarGridSpec(
            num_scalar_prefetch=1,
            grid=(deep,),
            in_specs=[pl.BlockSpec((1, *piece.shape[1:]), from_z) for piece in ins],
            out_specs=[
                pl.BlockSpec((1, 4, rows, width), lambda i, place: (i, 0, 0, 0))
                for width in widths
            ],
        ),
        out_shape=[
            jax.ShapeDtypeStruct((deep, 4, rows, width), jnp.bfloat16) for width in widths
        ],
        compiler_params=pltpu.CompilerParams(vmem_limit_bytes=48 * MEBI),
        cost_estimate=cost(
            flops=0, bytes_accessed=16 * deep * rows * sum(widths), transcendentals=0
        ),
    )(place.astype(jnp.int32), *ins)
    return [out.reshape(count * rows, out.shape[-1]) for out in outs]


def gather_small(shard):
    count = lax.axis_size("fsdp")
    deep = count // 4
    z, y, x = chip_place()
    both = jnp.stack([shard, lax.ppermute(shard, "fsdp", chip_flip(count, 2))])
    both = jnp.where(y == 0, both, both[::-1])
    four = jnp.stack([both, lax.ppermute(both, "fsdp", chip_flip(count, 1))], axis=1)
    four = jnp.where(x == 0, four, four[:, ::-1])
    blocks = [four] + [
        lax.ppermute(four, "fsdp", chip_shift(count, -step)) for step in range(1, deep)
    ]
    blocks = jnp.stack(blocks + blocks[:-1])
    blocks = lax.dynamic_slice_in_dim(blocks, lax.rem(deep - z, deep), deep, 0)
    return blocks.reshape(count * shard.shape[0], shard.shape[1])


def chip_place():
    chip = lax.axis_index("fsdp")
    return chip // 4, chip // 2 % 2, chip % 2


def picks(blocks, index, axis):
    return jnp.concatenate([pick(block, index, axis) for block in blocks], axis=-1)


def sum_first(terms, x_first):
    count = lax.axis_size("fsdp")
    _, y, x = chip_place()
    blocks = [
        term.reshape(count // 4, 2, 2, term.shape[0] // count, term.shape[1]) for term in terms
    ]
    return blocks, picks(blocks, 1 - x, 2) if x_first else picks(blocks, 1 - y, 1)


def across_chips(kept, gone, bit, earlier):
    came = lax.ppermute(gone, "fsdp", chip_flip(lax.axis_size("fsdp"), bit))
    return low(kept.astype(jnp.float32) + after(came, earlier).astype(jnp.float32))


def sum_second(blocks, gone, x_first, earlier):
    _, y, x = chip_place()
    kept = picks(blocks, x, 2) if x_first else picks(blocks, y, 1)
    sums = across_chips(kept, gone, 1 if x_first else 2, earlier)
    return sums, pick(sums, 1 - y if x_first else 1 - x, 1)


def sum_third(sums, gone, x_first, earlier):
    _, y, x = chip_place()
    return across_chips(pick(sums, y if x_first else x, 1), gone, 2 if x_first else 1, earlier)


def along_z(*columns):
    column = jnp.concatenate(columns, axis=-1)
    deep, z = column.shape[0], chip_place()[0]
    return column, [pick(column, lax.rem(z + step, deep), 0) for step in range(1, deep)]


def sum_last(column, gones, earlier):
    count = lax.axis_size("fsdp")
    total = pick(column, chip_place()[0], 0).astype(jnp.float32)
    for step, gone in enumerate(gones, 1):
        came = lax.ppermute(gone, "fsdp", chip_shift(count, step))
        total += after(came, earlier).astype(jnp.float32)
    return total


def tie(*values):
    return lax.optimization_barrier(values)


def after(value, earlier):
    return lax.optimization_barrier((value, earlier))[0]


def column_sum(rows):
    return jnp.sum(rows.astype(jnp.float32), axis=0, keepdims=True)


def body(
    tokens, timestep, text, cotangent, vectors, w_qkv, w_out, w_query2, w_kv2, w_out2, w_fc1, w_fc2
):
    cores = lax.axis_size("seq")
    images = tokens.shape[0]
    swap = cores == 2 and images == 2
    core = lax.axis_index("seq")
    other = 1 - core
    across = [(0, 1), (1, 0)]
    rows_here = w_fc1.shape[0]

    def trade(rows):
        mine = lax.dynamic_slice_in_dim(rows, core, 1, 0)
        gone = lax.dynamic_slice_in_dim(rows, other, 1, 0)
        return jnp.concatenate([mine, lax.ppermute(gone, "seq", across)], axis=1)

    def trade_back(rows):
        half = rows.shape[1] // 2
        return by_core(rows[:, :half], pair(rows[:, half:]), 0)

    def by_core(mine, came, axis):
        return jnp.where(
            core == 0,
            jnp.concatenate([mine, came], axis=axis),
            jnp.concatenate([came, mine], axis=axis),
        )

    def pair(part):
        return lax.ppermute(part, "seq", across)

    def mlp_shard():
        here = w_fc1.reshape(rows_here, -1, 2, 2, rows_here)
        gone, mine = pick(here, other, 2), pick(here, core, 2)
        first = by_core(mine, pair(gone), 1)
        first = first.transpose(0, 2, 1, 3).reshape(rows_here, -1)
        here = w_fc2.reshape(2, 2, rows_here, -1)
        gone, mine = pick(here, other, 0), pick(here, core, 0)
        second = by_core(mine, pair(gone), 2)
        return jnp.concatenate([first, second[0], second[1]], axis=1)

    def whole_rest(near, earlier):
        near = after(near, earlier)
        pieces = [*near, *far_pieces(near, 1408)]
        half = w_out.shape[1]
        return assemble(
            [pieces, [pair(piece) for piece in pieces]],
            [(0, half), (half, half), (2 * half, 2 * half), (4 * half, half)],
        )

    def gather_plain():
        whole = [
            lax.all_gather(
                lax.all_gather(part, "fsdp", axis=0, tiled=True), "seq", axis=1, tiled=True
            )
            for part in (w_qkv, w_out, w_query2, w_kv2, w_out2, w_fc1, w_fc2)
        ]
        first, second = whole[5:]
        mlp = [
            jnp.concatenate(
                [
                    first[:, 2 * part * D : 2 * (part + 1) * D],
                    second[2 * part * D : (2 * part + 1) * D],
                    second[(2 * part + 1) * D : 2 * (part + 1) * D],
                ],
                axis=1,
            )
            for part in range(2)
        ]
        return (*whole[:5], mlp)

    def core_parts(right):
        width = (right.shape[1] // 2 + 127) // 128 * 128
        low_part, high_part = right[:, :width], right[:, -width:]
        return (
            jnp.where(core == 0, high_part, low_part),
            jnp.where(core == 0, low_part, high_part),
        )

    def pair_send(left, right):
        return low(dot_tn(left, core_parts(right)[0]))

    def pair_sum(left, right, sent):
        return low(dot_tn(left, core_parts(right)[1]) + pair(sent).astype(jnp.float32))

    def pair_grad(left, right):
        return pair_sum(left, right, pair_send(left, right))

    def own_half(wide, place):
        return jnp.where(place == 0, wide[:, :-64], wide[:, 64:])

    def weight_grad(left, right):
        return scatter_plain(low(dot_tn(left, right)))

    def scatter_plain(full):
        part = lax.psum_scatter(full, "seq", scatter_dimension=1, tiled=True)
        return lax.psum_scatter(part, "fsdp", scatter_dimension=0, tiled=True).astype(jnp.float32)

    if swap:
        shard, vectors, tokens, text, cotangent = tie(
            mlp_shard(), vectors, tokens, text, cotangent
        )
        mlp_own = lax.all_gather(shard, "fsdp", axis=0, tiled=True)
        column = column_pieces(w_qkv)
        vec = gather_small(jnp.pad(vectors, ((0, 0), (0, 128 - vectors.shape[1]))))
        tokens, text, cotangent = trade(tokens), trade(text), trade(cotangent)
        column, vec, tokens, text, cotangent, others = tie(
            column, vec, tokens, text, cotangent, (w_out, w_query2, w_kv2, w_out2)
        )
        near = near_pieces(column)
        rest = column_pieces(jnp.concatenate(others, axis=1))
        far, rest = tie(far_pieces(near, 896), rest)
        rest_near = near_pieces(rest)
        pieces = [*near, *far]
        (wf_qkv,) = assemble([pieces, [pair(piece) for piece in pieces]], [(0, w_qkv.shape[1])])
        vec = vec.T[: vectors.shape[1]].astype(jnp.float32)
        timestep = lax.dynamic_slice_in_dim(timestep, core, 1, 0)
    batch, rows = tokens.shape[0], tokens.shape[1]
    if not swap:
        vec = lax.all_gather(vectors, "fsdp", axis=0, tiled=True).T.astype(jnp.float32)
        wf_qkv, wf_out, wf_query2, wf_kv2, wf_out2, mlp = gather_plain()

    def unflat(tensor):
        return tensor.reshape(batch, rows, tensor.shape[-1])

    inputs = tokens.astype(jnp.float32)
    modulation = vec[None, :6] + timestep.astype(jnp.float32).reshape(batch, 6, D)
    zero_bias = jnp.zeros((1, D), jnp.float32)
    h_attn = lax.optimization_barrier(
        low(modulated(inputs, modulation[:, 0:1], modulation[:, 1:2]))
    )
    qkv_bias = jnp.concatenate([vec[6:7], zero_bias, vec[7:8]], axis=1)
    qkv_rows = unflat(low(matmul(flatten(h_attn), wf_qkv) + qkv_bias))
    if swap:
        self_qkv = ((qkv_rows, 0), (qkv_rows, 1), (qkv_rows, 2))
    else:
        all_kv = lax.all_gather(qkv_rows[..., D:], "seq", axis=1, tiled=True)
        self_qkv = ((qkv_rows, 0), (all_kv, 0), (all_kv, 1))
    attn_low, self_lse = attend_forward(*self_qkv, 512)
    if swap:
        wf_out, wf_query2, wf_kv2, wf_out2 = whole_rest(rest_near, attn_low)
    attn_proj, after_attn, after_low, cross_query = self_output(
        attn_low, wf_out, vec[8:9], tokens, modulation[:, 2:3], wf_query2, vec[9:10]
    )
    kv_bias = jnp.concatenate([zero_bias, vec[10:11]], axis=1)
    text_kv = low(matmul(flatten(text), wf_kv2) + kv_bias).reshape(batch, text.shape[1], 2 * D)
    if not swap:
        text_kv = lax.all_gather(text_kv, "seq", axis=1, tiled=True)
    cross_qkv = ((cross_query, 0), (text_kv, 0), (text_kv, 1))
    cross_low, cross_lse = attend_forward(*cross_qkv, 1024)
    after_cross, h_mlp = cross_output(
        cross_low, wf_out2, vec[11:12], after_attn, modulation[:, 3:4], modulation[:, 4:5]
    )
    fc1_bias = vec[13:].reshape(1, -1)
    if swap:
        fc1_bias = fc1_bias.reshape(-1, 2, 2, rows_here)
        biases = [
            pick(fc1_bias, place, 1).transpose(1, 0, 2).reshape(1, -1) for place in (core, other)
        ]
    else:
        biases = [fc1_bias[:, : 2 * D], fc1_bias[:, 2 * D :]]
    if swap:
        mlp = (mlp_own, pair(after(mlp_own, h_mlp)))
    hidden = [mlp_first(h_mlp, whole, bias) for whole, bias in zip(mlp, biases)]
    lows = [hidden_low for hidden_low, _ in hidden]
    result, grad_mlp, grad_gate_mlp, fc2_sums = mlp_second(
        lows, mlp, vec[12:13], after_cross, modulation[:, 5:6], cotangent
    )

    flat_h, flat_gm = flatten(h_mlp), flatten(grad_mlp)
    if swap:
        own_low, other_low = flatten(lows[0]), flatten(lows[1])
        sent = low(dot_tn(other_low, flat_gm))
        sent, grad_mlp = tie(sent, grad_mlp)
        other_pre, other_sums = mlp_slope(grad_mlp, mlp[1], hidden[1][1])
        fc2_part = low(dot_tn(own_low, flat_gm) + pair(sent).astype(jnp.float32))
        fc2_x, fc2_gone_x = sum_first([fc2_part[:D]], True)
        fc2_y, fc2_gone_y = sum_first([fc2_part[D:]], False)
        fc2_gone_x, fc2_gone_y, other_pre, grad_mlp = tie(
            fc2_gone_x, fc2_gone_y, other_pre, grad_mlp
        )
        sent = low(dot_tn(flat_h, flatten(other_pre)))
        sent, grad_mlp = tie(sent, grad_mlp)
        own_pre, own_sums = mlp_slope(grad_mlp, mlp[0], hidden[0][1])
        fc2_x, fc2_gone_x = sum_second(fc2_x, fc2_gone_x, True, own_pre)
        fc2_y, fc2_gone_y = sum_second(fc2_y, fc2_gone_y, False, own_pre)
        fc2_gone_x, fc2_gone_y, own_pre = tie(fc2_gone_x, fc2_gone_y, own_pre)
        fc1_part = low(dot_tn(flat_h, flatten(own_pre)) + pair(sent).astype(jnp.float32))
        fc1_x, fc1_gone_x = sum_first([fc1_part[:, :D]], True)
        fc1_y, fc1_gone_y = sum_first([fc1_part[:, D:]], False)
        own_pre, fc1_gone_x, fc1_gone_y = tie(own_pre, fc1_gone_x, fc1_gone_y)
        result = after(result, fc1_gone_x)
        grads_pre, fc1_sums = [own_pre, other_pre], [own_sums, other_sums]
    else:
        slopes = [mlp_slope(grad_mlp, whole, slope) for whole, (_, slope) in zip(mlp, hidden)]
        grads_pre = [grad_pre for grad_pre, _ in slopes]
        fc1_sums = [sums for _, sums in slopes]
    fc1_sums = [jnp.sum(sums, axis=0) for sums in fc1_sums]
    grad_cross, grad_proj2, grad_shift_mlp, grad_scale_mlp, out2_sums = mlp_input(
        grads_pre, mlp, after_cross, modulation[:, 4:5], cotangent
    )
    grad_proj2 = flatten(grad_proj2)
    if swap:
        fc1_x, fc1_gone_x = sum_second(fc1_x, fc1_gone_x, True, grad_proj2)
        fc1_y, fc1_gone_y = sum_second(fc1_y, fc1_gone_y, False, grad_proj2)
        fc1_gone_x, fc1_gone_y, grad_proj2 = tie(fc1_gone_x, fc1_gone_y, grad_proj2)
    grad_mixed2 = unflat(low(dot_nt(grad_proj2, wf_out2)))
    if swap:
        out2_part = pair_grad(flatten(cross_low), grad_proj2)
        grad_mixed2, out2_part = tie(grad_mixed2, out2_part)
    grad_q2, grad_kv = attend_backward(
        *cross_qkv, grad_mixed2, cross_low, cross_lse, 1024, False,
        jnp.bfloat16 if swap else jnp.float32,
    )
    if not swap:
        grad_kv = low(lax.psum_scatter(grad_kv, "seq", scatter_dimension=1, tiled=True))
    grad_kv, grad_q2 = flatten(grad_kv), flatten(grad_q2)
    if swap:
        mlp_column, mlp_gones = along_z(
            sum_third(fc1_x, fc1_gone_x, True, grad_q2),
            sum_third(fc1_y, fc1_gone_y, False, grad_q2),
            sum_third(fc2_x, fc2_gone_x, True, grad_q2),
            sum_third(fc2_y, fc2_gone_y, False, grad_q2),
        )
        mlp_gones, grad_q2, grad_kv = tie(mlp_gones, grad_q2, grad_kv)
    grad_text = dot_nt(grad_kv, wf_kv2).reshape(text.shape)
    grad_attn = grad_cross + unflat(dot_nt(grad_q2, wf_query2))
    grad_gate_attn = jnp.sum(grad_attn * attn_proj, axis=1, keepdims=True)
    grad_proj1 = flatten(low(modulation[:, 2:3] * grad_attn))
    grad_mixed1 = unflat(low(dot_nt(grad_proj1, wf_out)))
    if swap:
        rest_x, gone_x = sum_first(
            [
                pair_grad(flatten(text), grad_kv),
                pair_grad(flatten(attn_low), grad_proj1),
            ],
            True,
        )
        rest_y, gone_y = sum_first(
            [out2_part, pair_grad(flatten(after_low), grad_q2)], False
        )
        gone_x, gone_y, grad_mixed1 = tie(gone_x, gone_y, grad_mixed1)
        (grad_qkv_low,) = attend_backward(
            *self_qkv, grad_mixed1, attn_low, self_lse, 256, True, jnp.bfloat16
        )
        grad_qkv_low = flatten(grad_qkv_low)
        rest_x, gone_x = sum_second(rest_x, gone_x, True, grad_qkv_low)
        rest_y, gone_y = sum_second(rest_y, gone_y, False, grad_qkv_low)
        mlp_part = sum_last(mlp_column, mlp_gones, grad_qkv_low)
        gone_x, gone_y, mlp_part, grad_qkv_low = tie(gone_x, gone_y, mlp_part, grad_qkv_low)
        qkv_part = pair_grad(flatten(h_attn), grad_qkv_low)
        columns = qkv_part.shape[1] // 2
        qkv_x, qkv_gone_x = sum_first([qkv_part[:, :columns]], True)
        qkv_y, qkv_gone_y = sum_first([qkv_part[:, columns:]], False)
        column, gones = along_z(
            sum_third(rest_x, gone_x, True, qkv_gone_x),
            sum_third(rest_y, gone_y, False, qkv_gone_y),
        )
        gones, qkv_gone_x, qkv_gone_y, grad_qkv_low = tie(
            gones, qkv_gone_x, qkv_gone_y, grad_qkv_low
        )
        grad_tokens, grad_shift_attn, grad_scale_attn, qkv_sums = attend_input(
            unflat(grad_qkv_low), wf_qkv, tokens, modulation[:, 1:2], grad_attn
        )
        qkv_x, gone_x = sum_second(qkv_x, qkv_gone_x, True, grad_shift_attn)
        qkv_y, gone_y = sum_second(qkv_y, qkv_gone_y, False, grad_shift_attn)
        gone_x, gone_y, grad_tokens, grad_shift_attn, grad_scale_attn, qkv_sums = tie(
            gone_x, gone_y, grad_tokens, grad_shift_attn, grad_scale_attn, qkv_sums
        )
        rest = sum_last(column, gones, gone_x)
        column, gones = along_z(
            sum_third(qkv_x, gone_x, True, rest), sum_third(qkv_y, gone_y, False, rest)
        )
        grad_qkv = own_half(sum_last(column, gones, rest), core)
        mlp_part, grad_text = after((mlp_part, grad_text), gones[0])
        grad_kv2 = rest[:, : 2 * w_out.shape[1]]
        grad_out, grad_out2, grad_query2 = [
            own_half(part, core) for part in jnp.split(rest[:, grad_kv2.shape[1] :], 3, axis=1)
        ]
        here = mlp_part[:, : 2 * D].reshape(rows_here, 2, -1, rows_here).transpose(0, 2, 1, 3)
        here = here.reshape(rows_here, 2, -1, 2, rows_here)
        gone, mine = pick(here, other, 1), pick(here, core, 1)
        grad_fc1 = by_core(mine[:, :, None], pair(gone)[:, :, None], 2).reshape(w_fc1.shape)
        here = jnp.concatenate([mlp_part[:, 2 * D : 3 * D], mlp_part[:, 3 * D :]], axis=0)
        gone, mine = core_parts(here)
        gone, mine = own_half(gone, other), own_half(mine, core)
        grad_fc2 = by_core(mine, pair(gone), 0)
        fc1_sums = by_core(fc1_sums[0], fc1_sums[1], 1).reshape(2, 2, -1, rows_here)
        fc1_sums = fc1_sums.transpose(2, 0, 1, 3)
    else:
        grad_q, grad_kv1 = attend_backward(
            *self_qkv, grad_mixed1, attn_low, self_lse, 256, False, jnp.float32
        )
        grad_kv1 = lax.psum_scatter(grad_kv1, "seq", scatter_dimension=1, tiled=True)
        grad_qkv_low = flatten(jnp.concatenate([grad_q, low(grad_kv1)], axis=-1))
        grad_tokens, grad_shift_attn, grad_scale_attn, qkv_sums = attend_input(
            unflat(grad_qkv_low), wf_qkv, tokens, modulation[:, 1:2], grad_attn
        )
        grad_fc1 = scatter_plain(
            jnp.concatenate([low(dot_tn(flat_h, flatten(part))) for part in grads_pre], axis=1)
        )
        grad_fc2 = scatter_plain(
            jnp.concatenate([low(dot_tn(flatten(part), flat_gm)) for part in lows], axis=0)
        )
        grad_out2 = weight_grad(flatten(cross_low), grad_proj2)
        grad_kv2 = weight_grad(flatten(text), grad_kv)
        grad_query2 = weight_grad(flatten(after_low), grad_q2)
        grad_out = weight_grad(flatten(attn_low), grad_proj1)
        grad_qkv = weight_grad(flatten(h_attn), grad_qkv_low)
        fc1_sums = jnp.concatenate(fc1_sums, axis=1)
    grad_time = jnp.concatenate(
        [
            grad_shift_attn,
            grad_scale_attn,
            grad_gate_attn,
            grad_shift_mlp,
            grad_scale_mlp,
            grad_gate_mlp,
        ],
        axis=1,
    )
    qkv_sums = jnp.sum(qkv_sums, axis=0)
    grad_vectors = jnp.concatenate(
        [
            jnp.sum(grad_time, axis=0),
            qkv_sums[:, :D],
            qkv_sums[:, 2 * D :],
            column_sum(grad_proj1),
            column_sum(grad_q2),
            column_sum(grad_kv[:, D:]),
            jnp.sum(out2_sums, axis=0),
            jnp.sum(fc2_sums, axis=0),
            fc1_sums.reshape(-1, D),
        ],
        axis=0,
    ).T
    if swap:
        count = grad_vectors.shape[1]
        part = low(jnp.pad(grad_vectors, ((0, 0), (0, 128 - count))))
        part = low(part.astype(jnp.float32) + pair(part).astype(jnp.float32))
        blocks, gone = sum_first([part], True)
        sums, gone = sum_second(blocks, gone, True, part)
        part = sum_last(*along_z(sum_third(sums, gone, True, part)), part)
        grad_vectors = part[:, :count]
    else:
        grad_vectors = lax.psum_scatter(
            lax.psum(grad_vectors, "seq"), "fsdp", scatter_dimension=0, tiled=True
        )
    grad_time = grad_time.reshape(batch, 6 * D)
    if swap:
        grad_time = by_core(grad_time, pair(grad_time), 0)
        result, grad_tokens, grad_text = (
            trade_back(result), trade_back(grad_tokens), trade_back(grad_text),
        )
    else:
        grad_time = lax.psum(grad_time, "seq")
    return (
        result,
        grad_tokens,
        grad_time,
        grad_text,
        grad_vectors,
        grad_qkv,
        grad_out,
        grad_query2,
        grad_kv2,
        grad_out2,
        grad_fc1,
        grad_fc2,
    )


def solution(mesh):
    in_specs = (
        P("fsdp", "seq", None),
        P("fsdp", None),
        P("fsdp", "seq", None),
        P("fsdp", "seq", None),
        P("fsdp", None),
        P("fsdp", "seq"),
        P("fsdp", "seq"),
        P("fsdp", "seq"),
        P("fsdp", "seq"),
        P("fsdp", "seq"),
        P("fsdp", "seq"),
        P("fsdp", "seq"),
    )
    out_specs = (
        P("fsdp", "seq", None),
        P("fsdp", "seq", None),
        P("fsdp", None),
        P("fsdp", "seq", None),
        P("fsdp", None),
        P("fsdp", "seq"),
        P("fsdp", "seq"),
        P("fsdp", "seq"),
        P("fsdp", "seq"),
        P("fsdp", "seq"),
        P("fsdp", "seq"),
        P("fsdp", "seq"),
    )
    return jax.shard_map(body, mesh=mesh, in_specs=in_specs, out_specs=out_specs, check_vma=False)
```

```python
import functools

import jax
import jax.numpy as jnp
from jax import lax
from jax.experimental import pallas as pl
from jax.experimental.pallas import tpu as pltpu
from jax.sharding import PartitionSpec as P

D = 1152
HEADS = 16
HEAD_DIM = 72
MEBI = 1024 * 1024
VMEM_LIMIT = 56 * MEBI
COST_SHARE = 1000

norm_eps = 1e-06
gelu_root = 0.7978845608028654
gelu_cube = 0.044715


def norm_rows(inputs):
    center = inputs - jnp.mean(inputs, axis=-1, keepdims=True)
    spread = jnp.mean(center * center, axis=-1, keepdims=True)
    return center * lax.rsqrt(spread + norm_eps)


def gelu_tanh(inputs):
    return (
        0.5 * inputs * (1.0 + jnp.tanh(gelu_root * (inputs + gelu_cube * inputs * inputs * inputs)))
    )


def modulated(inputs, shift_rows, scale_rows):
    return norm_rows(inputs) * (1.0 + scale_rows) + shift_rows


def flatten(tensor):
    return tensor.reshape(-1, tensor.shape[-1])


def low(values):
    return values.astype(jnp.bfloat16)


def dot_nt(left, right):
    return lax.dot_general(left, right, (((1,), (1,)), ((), ())), preferred_element_type=jnp.float32)


def dot_tn(left, right):
    return lax.dot_general(left, right, (((0,), (0,)), ((), ())), preferred_element_type=jnp.float32)


def cost(flops, bytes_accessed, transcendentals):
    return pl.CostEstimate(
        flops=flops // COST_SHARE,
        bytes_accessed=bytes_accessed // COST_SHARE,
        transcendentals=transcendentals // COST_SHARE,
    )


LANES = 256
LOG2E = 1.4426950408889634
SCALE = HEAD_DIM**-0.5


def contract_last(left, right):
    return lax.dot_general(left, right, (((1,), (1,)), ((), ())), preferred_element_type=jnp.float32)


def matmul(left, right):
    return jnp.dot(left, right, preferred_element_type=jnp.float32)


def head_window(head):
    first = head * HEAD_DIM
    start = pl.multiple_of(jnp.minimum(first // 128 * 128, D - LANES), 128)
    column = start + lax.broadcasted_iota(jnp.int32, (1, LANES), 1)
    inside = (column >= first) & (column < first + HEAD_DIM)
    return pl.ds(start, LANES), inside


def fill_transposed(rows_ref, columns_scr):
    columns_scr[...] = jnp.transpose(rows_ref[0].astype(jnp.float32)).astype(jnp.bfloat16)


def aligned_rows(pair, odd):
    return pl.ds(pl.multiple_of(pair * 144 + 64 * odd, 16), 80)


def head_rows(head):
    return pl.ds(pl.multiple_of(head * HEAD_DIM, 8), HEAD_DIM)


def for_heads(ahead, then):
    ahead(0, 0)

    def two_heads(pair, carry):
        ahead(2 * pair + 1, 1)
        then(2 * pair, pair, 0)
        ahead(jnp.minimum(2 * pair + 2, HEADS - 1), 0)
        then(2 * pair + 1, pair, 1)
        return carry

    lax.fori_loop(0, HEADS // 2, two_heads, 0)


def attend_forward_kernel(q_ref, k_ref, v_ref, o_ref, lse_ref, vt_scr, ot_scr, s_scr):
    @pl.when(pl.program_id(1) == 0)
    def _():
        fill_transposed(v_ref, vt_scr)

    def ahead(head, slot):
        window, inside = head_window(head)
        q_head = q_ref[0, :, window] * inside.astype(jnp.bfloat16)
        s_scr[slot] = contract_last(k_ref[0, :, window], q_head)

    def then(head, pair, slot):
        scores = s_scr[slot]
        top = jnp.max(scores, axis=0, keepdims=True)
        weights = jnp.exp2((scores - top) * (SCALE * LOG2E))
        total = jnp.sum(weights, axis=0, keepdims=True)
        mixed = matmul(vt_scr[aligned_rows(pair, slot), :], weights.astype(jnp.bfloat16))
        ot_scr[head_rows(head), :] = mixed[8 * slot : 8 * slot + HEAD_DIM] * (1.0 / total)
        lse_ref[0, pl.ds(head, 1), :] = top * (SCALE * LOG2E) + jnp.log2(total)

    for_heads(ahead, then)
    o_ref[0] = jnp.transpose(ot_scr[...]).astype(jnp.bfloat16)


def attend_forward(queries, keys, values, row_block):
    (q_arr, q_blk), (k_arr, k_blk), (v_arr, v_blk) = queries, keys, values
    batch, rows, key_rows = q_arr.shape[0], q_arr.shape[1], k_arr.shape[1]
    block = min(row_block, rows)
    return pl.pallas_call(
        attend_forward_kernel,
        grid=(batch, rows // block),
        in_specs=[
            pl.BlockSpec((1, block, D), lambda b, i: (b, i, q_blk)),
            pl.BlockSpec((1, key_rows, D), lambda b, i: (b, 0, k_blk)),
            pl.BlockSpec((1, key_rows, D), lambda b, i: (b, 0, v_blk)),
        ],
        out_specs=[
            pl.BlockSpec((1, block, D), lambda b, i: (b, i, 0)),
            pl.BlockSpec((1, HEADS, block), lambda b, i: (b, 0, i)),
        ],
        out_shape=[
            jax.ShapeDtypeStruct((batch, rows, D), jnp.bfloat16),
            jax.ShapeDtypeStruct((batch, HEADS, rows), jnp.float32),
        ],
        scratch_shapes=[
            pltpu.VMEM((D, key_rows), jnp.bfloat16),
            pltpu.VMEM((D, block), jnp.float32),
            pltpu.VMEM((2, key_rows, block), jnp.float32),
        ],
        compiler_params=pltpu.CompilerParams(vmem_limit_bytes=48 * MEBI),
        cost_estimate=cost(
            flops=4 * batch * rows * key_rows * HEADS * LANES,
            bytes_accessed=4 * batch * (rows + key_rows) * D,
            transcendentals=batch * rows * key_rows * HEADS,
        ),
    )(q_arr, k_arr, v_arr)


def attend_backward_kernel(
    fused, q_ref, k_ref, v_ref, g_ref, o_ref, lse_ref, *rest
):
    if fused:
        out_ref, kt_scr, dk_scr, dv_scr, dqt_scr, dot_scr, s_scr, g_scr = rest
    else:
        dq_ref, dkv_ref, kt_scr, dk_scr, dv_scr, dqt_scr, dot_scr, s_scr, g_scr = rest
    step = pl.program_id(1)
    block = q_ref.shape[1]

    @pl.when(step == 0)
    def _():
        fill_transposed(k_ref, kt_scr)
        dk_scr[...] = jnp.zeros_like(dk_scr)
        dv_scr[...] = jnp.zeros_like(dv_scr)

    products = g_ref[0].astype(jnp.float32) * o_ref[0].astype(jnp.float32)
    head_row = lax.broadcasted_iota(jnp.int32, (HEADS, D), 0) * HEAD_DIM
    column = lax.broadcasted_iota(jnp.int32, (HEADS, D), 1)
    member = ((column >= head_row) & (column < head_row + HEAD_DIM)).astype(jnp.bfloat16)
    high = products.astype(jnp.bfloat16)
    rest_low = (products - high.astype(jnp.float32)).astype(jnp.bfloat16)
    dot_scr[...] = contract_last(member, high) + contract_last(member, rest_low)

    def masked(ref, head):
        window, inside = head_window(head)
        return ref[0, :, window] * inside.astype(jnp.bfloat16)

    def ahead(head, slot):
        window, _ = head_window(head)
        s_scr[slot] = contract_last(k_ref[0, :, window], masked(q_ref, head))
        g_scr[slot] = contract_last(v_ref[0, :, window], masked(g_ref, head))

    def then(head, pair, slot):
        window, _ = head_window(head)
        row = pl.ds(head, 1)
        weights = jnp.exp2(s_scr[slot] * (SCALE * LOG2E) - lse_ref[0, row, :])
        grad_scores = (weights * (g_scr[slot] - dot_scr[row, :])).astype(jnp.bfloat16)
        dv_scr[:, window] += matmul(weights.astype(jnp.bfloat16), masked(g_ref, head))
        dk_scr[:, window] += matmul(grad_scores, masked(q_ref, head))
        dq_rows = matmul(kt_scr[aligned_rows(pair, slot), :], grad_scores)
        dqt_scr[head_rows(head), :] = dq_rows[8 * slot : 8 * slot + HEAD_DIM]

    for_heads(ahead, then)
    grad_q = (jnp.transpose(dqt_scr[...]) * SCALE).astype(jnp.bfloat16)
    if fused:
        out_ref[0, pl.ds(pl.multiple_of(step * block, block), block), :D] = grad_q
    else:
        dq_ref[0] = grad_q

    @pl.when(step == pl.num_programs(1) - 1)
    def _():
        if fused:
            out_ref[0, :, D : 2 * D] = (dk_scr[...] * SCALE).astype(out_ref.dtype)
            out_ref[0, :, 2 * D :] = dv_scr[...].astype(out_ref.dtype)
        else:
            dkv_ref[0, :, :D] = (dk_scr[...] * SCALE).astype(dkv_ref.dtype)
            dkv_ref[0, :, D:] = dv_scr[...].astype(dkv_ref.dtype)


def attend_backward(queries, keys, values, grad_mixed, mixed, lse, row_block, fused, kv_dtype):
    (q_arr, q_blk), (k_arr, k_blk), (v_arr, v_blk) = queries, keys, values
    batch, rows, key_rows = q_arr.shape[0], q_arr.shape[1], k_arr.shape[1]
    block = min(row_block, rows)
    if fused:
        out_specs = [pl.BlockSpec((1, key_rows, 3 * D), lambda b, i: (b, 0, 0))]
        out_shape = [jax.ShapeDtypeStruct((batch, key_rows, 3 * D), jnp.bfloat16)]
    else:
        out_specs = [
            pl.BlockSpec((1, block, D), lambda b, i: (b, i, 0)),
            pl.BlockSpec((1, key_rows, 2 * D), lambda b, i: (b, 0, 0)),
        ]
        out_shape = [
            jax.ShapeDtypeStruct((batch, rows, D), jnp.bfloat16),
            jax.ShapeDtypeStruct((batch, key_rows, 2 * D), kv_dtype),
        ]
    return pl.pallas_call(
        functools.partial(attend_backward_kernel, fused),
        grid=(batch, rows // block),
        in_specs=[
            pl.BlockSpec((1, block, D), lambda b, i: (b, i, q_blk)),
            pl.BlockSpec((1, key_rows, D), lambda b, i: (b, 0, k_blk)),
            pl.BlockSpec((1, key_rows, D), lambda b, i: (b, 0, v_blk)),
            pl.BlockSpec((1, block, D), lambda b, i: (b, i, 0)),
            pl.BlockSpec((1, block, D), lambda b, i: (b, i, 0)),
            pl.BlockSpec((1, HEADS, block), lambda b, i: (b, 0, i)),
        ],
        out_specs=out_specs,
        out_shape=out_shape,
        scratch_shapes=[
            pltpu.VMEM((D, key_rows), jnp.bfloat16),
            pltpu.VMEM((key_rows, D), jnp.float32),
            pltpu.VMEM((key_rows, D), jnp.float32),
            pltpu.VMEM((D, block), jnp.float32),
            pltpu.VMEM((HEADS, block), jnp.float32),
            pltpu.VMEM((2, key_rows, block), jnp.float32),
            pltpu.VMEM((2, key_rows, block), jnp.float32),
        ],
        compiler_params=pltpu.CompilerParams(vmem_limit_bytes=VMEM_LIMIT),
        cost_estimate=cost(
            flops=10 * batch * rows * key_rows * HEADS * LANES,
            bytes_accessed=2 * batch * (3 * rows + 2 * key_rows + 3 * key_rows) * D,
            transcendentals=batch * rows * key_rows * HEADS,
        ),
    )(q_arr, k_arr, v_arr, grad_mixed, mixed, lse)


MLP_TILE = 768


def row_chunks(rows, most=256):
    size = min(most, rows)
    return [slice(first, first + size) for first in range(0, rows, size)]


def lagged(rows, product, use, most=256):
    waiting = None
    for part in row_chunks(rows, most):
        value = product(part)
        if waiting is not None:
            use(*waiting)
        waiting = (part, value)
    use(*waiting)


def mlp_first_kernel(h_ref, w_ref, b_ref, low_ref, slope_ref):
    def product(part):
        return matmul(h_ref[0, part], w_ref[...])

    def use(part, value):
        value = value + b_ref[...]
        square = value * value
        bent = jnp.tanh(value * (gelu_root * gelu_cube * square + gelu_root))
        half = 0.5 * value
        low_ref[0, part] = low(half * bent + half)
        inner = 3.0 * gelu_root * gelu_cube * square + gelu_root
        slope_ref[0, part] = low(half * inner * (1.0 - bent * bent) + (0.5 * bent + 0.5))

    lagged(h_ref.shape[1], product, use)


def mlp_first(h_mlp, whole, bias):
    batch, rows = h_mlp.shape[:2]
    tile = pl.BlockSpec((1, rows, MLP_TILE), lambda b, i: (b, 0, i))
    shape = jax.ShapeDtypeStruct((batch, rows, 2 * D), jnp.bfloat16)
    return pl.pallas_call(
        mlp_first_kernel,
        grid=(batch, 2 * D // MLP_TILE),
        in_specs=[
            pl.BlockSpec((1, rows, D), lambda b, i: (b, 0, 0)),
            pl.BlockSpec((D, MLP_TILE), lambda b, i: (0, i)),
            pl.BlockSpec((1, MLP_TILE), lambda b, i: (0, i)),
        ],
        out_specs=[tile, tile],
        out_shape=[shape, shape],
        compiler_params=pltpu.CompilerParams(vmem_limit_bytes=VMEM_LIMIT),
        cost_estimate=cost(
            flops=4 * batch * rows * D * D,
            bytes_accessed=2 * (batch * rows * 5 * D + 2 * D * D),
            transcendentals=2 * batch * rows * D,
        ),
    )(h_mlp, whole, bias)


def mlp_second_kernel(
    lo_ref, lc_ref, wo_ref, wc_ref, b_ref, x_ref, gate_ref, e_ref,
    out_ref, gm_ref, gate_sum_ref, gm_sum_ref, acc_scr,
):
    step = pl.program_id(1)

    @pl.when(step == 0)
    def _():
        acc_scr[...] = matmul(lo_ref[0], wo_ref[...])

    @pl.when(step == 1)
    def _():
        acc_scr[...] += matmul(lo_ref[0], wo_ref[...])

    @pl.when(step == 2)
    def _():
        acc_scr[...] += matmul(lc_ref[0], wc_ref[...])

    @pl.when(step == 3)
    def _():
        gate = gate_ref[0]
        sums = [0.0, 0.0]

        def product(part):
            return acc_scr[part] + matmul(lc_ref[0, part], wc_ref[...])

        def use(part, value):
            mlp_out = value + b_ref[...]
            grad = e_ref[0, part].astype(jnp.float32)
            out_ref[0, part] = low(x_ref[0, part] + gate * mlp_out)
            grad_mlp = low(gate * grad)
            gm_ref[0, part] = grad_mlp
            sums[0] += jnp.sum(grad * mlp_out, axis=0, keepdims=True)
            sums[1] += jnp.sum(grad_mlp.astype(jnp.float32), axis=0, keepdims=True)

        lagged(lo_ref.shape[1], product, use)
        gate_sum_ref[0], gm_sum_ref[0] = sums


def mlp_second(lows, wholes, bias, after_cross, gate, cotangent):
    batch, rows = after_cross.shape[:2]
    full = pl.BlockSpec((1, rows, D), lambda b, k: (b, 0, 0))
    row = pl.BlockSpec((1, 1, D), lambda b, k: (b, 0, 0))

    def first(k):
        return jnp.minimum(k, 1)

    def later(k):
        return jnp.maximum(k - 2, 0)

    return pl.pallas_call(
        mlp_second_kernel,
        grid=(batch, 4),
        in_specs=[
            pl.BlockSpec((1, rows, D), lambda b, k: (b, 0, first(k))),
            pl.BlockSpec((1, rows, D), lambda b, k: (b, 0, later(k))),
            pl.BlockSpec((D, D), lambda b, k: (0, 2 + first(k))),
            pl.BlockSpec((D, D), lambda b, k: (0, 2 + later(k))),
            pl.BlockSpec((1, D), lambda b, k: (0, 0)),
            full,
            row,
            full,
        ],
        out_specs=[full, full, row, row],
        out_shape=[
            jax.ShapeDtypeStruct((batch, rows, D), jnp.bfloat16),
            jax.ShapeDtypeStruct((batch, rows, D), jnp.bfloat16),
            jax.ShapeDtypeStruct((batch, 1, D), jnp.float32),
            jax.ShapeDtypeStruct((batch, 1, D), jnp.float32),
        ],
        scratch_shapes=[pltpu.VMEM((rows, D), jnp.float32)],
        compiler_params=pltpu.CompilerParams(vmem_limit_bytes=56 * MEBI),
        cost_estimate=cost(
            flops=8 * batch * rows * D * D,
            bytes_accessed=batch * rows * D * 18 + 8 * D * D,
            transcendentals=0,
        ),
    )(*lows, *wholes, bias, after_cross, gate, cotangent)


def mlp_slope_kernel(g_ref, w_ref, slope_ref, gp_ref, sum_ref):
    sums = [0.0]

    def product(part):
        return contract_last(g_ref[0, part], w_ref[...])

    def use(part, value):
        grad = low(value * slope_ref[0, part].astype(jnp.float32))
        gp_ref[0, part] = grad
        sums[0] += jnp.sum(grad.astype(jnp.float32), axis=0, keepdims=True)

    lagged(g_ref.shape[1], product, use)
    sum_ref[0] = sums[0]


def mlp_slope(grad_mlp, whole, slope):
    batch, rows = grad_mlp.shape[:2]
    return pl.pallas_call(
        mlp_slope_kernel,
        grid=(batch, 2),
        in_specs=[
            pl.BlockSpec((1, rows, D), lambda b, i: (b, 0, 0)),
            pl.BlockSpec((D, D), lambda b, i: (0, 2 + i)),
            pl.BlockSpec((1, rows, D), lambda b, i: (b, 0, i)),
        ],
        out_specs=[
            pl.BlockSpec((1, rows, D), lambda b, i: (b, 0, i)),
            pl.BlockSpec((1, 1, D), lambda b, i: (b, 0, i)),
        ],
        out_shape=[
            jax.ShapeDtypeStruct((batch, rows, 2 * D), jnp.bfloat16),
            jax.ShapeDtypeStruct((batch, 1, 2 * D), jnp.float32),
        ],
        compiler_params=pltpu.CompilerParams(vmem_limit_bytes=42 * MEBI),
        cost_estimate=cost(
            flops=4 * batch * rows * D * D,
            bytes_accessed=2 * (batch * rows * 5 * D + 2 * D * D),
            transcendentals=0,
        ),
    )(grad_mlp, whole, slope)


def norm_backward(inputs, grad, scale_rows):
    center = inputs - jnp.mean(inputs, axis=-1, keepdims=True)
    spread = jnp.mean(center * center, axis=-1, keepdims=True)
    root = lax.rsqrt(spread + norm_eps)
    normed = center * root
    grad_shift = jnp.sum(grad, axis=0, keepdims=True)
    grad_scale = jnp.sum(grad * normed, axis=0, keepdims=True)
    inner = grad * (1.0 + scale_rows)
    along = jnp.mean(inner * normed, axis=-1, keepdims=True)
    inner = root * (inner - jnp.mean(inner, axis=-1, keepdims=True) - normed * along)
    return inner, grad_shift, grad_scale


def mlp_input_kernel(
    go_ref, gc_ref, wo_ref, wc_ref, x_ref, scale_ref, e_ref,
    gx_ref, gl_ref, shift_sum_ref, scale_sum_ref, gl_sum_ref, acc_scr,
):
    step = pl.program_id(1)

    @pl.when(step == 0)
    def _():
        acc_scr[...] = jnp.zeros_like(acc_scr)

    @pl.when(step < 3)
    def _():
        acc_scr[...] += contract_last(go_ref[0], wo_ref[...])

    @pl.when((step >= 3) & (step < 5))
    def _():
        acc_scr[...] += contract_last(gc_ref[0], wc_ref[...])

    @pl.when(step == 5)
    def _():
        sums = [0.0, 0.0, 0.0]

        def product(part):
            return acc_scr[part] + contract_last(gc_ref[0, part], wc_ref[...])

        def use(part, grad):
            inner, grad_shift, grad_scale = norm_backward(x_ref[0, part], grad, scale_ref[0])
            inner += e_ref[0, part].astype(jnp.float32)
            gx_ref[0, part] = inner
            gl_ref[0, part] = low(inner)
            low_sum = jnp.sum(low(inner).astype(jnp.float32), axis=0, keepdims=True)
            for at, new in enumerate((grad_shift, grad_scale, low_sum)):
                sums[at] += new

        lagged(go_ref.shape[1], product, use)
        shift_sum_ref[0], scale_sum_ref[0], gl_sum_ref[0] = sums


def mlp_input(grads, wholes, after_cross, scale_rows, cotangent):
    batch, rows = after_cross.shape[:2]
    full = pl.BlockSpec((1, rows, D), lambda b, k: (b, 0, 0))
    row = pl.BlockSpec((1, 1, D), lambda b, k: (b, 0, 0))
    row_shape = jax.ShapeDtypeStruct((batch, 1, D), jnp.float32)

    def first(k):
        return jnp.minimum(k, 2)

    def later(k):
        return jnp.maximum(k - 3, 0)

    return pl.pallas_call(
        mlp_input_kernel,
        grid=(batch, 6),
        in_specs=[
            pl.BlockSpec((1, rows, MLP_TILE), lambda b, k: (b, 0, first(k))),
            pl.BlockSpec((1, rows, MLP_TILE), lambda b, k: (b, 0, later(k))),
            pl.BlockSpec((D, MLP_TILE), lambda b, k: (0, first(k))),
            pl.BlockSpec((D, MLP_TILE), lambda b, k: (0, later(k))),
            full,
            row,
            full,
        ],
        out_specs=[full, full, row, row, row],
        out_shape=[
            jax.ShapeDtypeStruct((batch, rows, D), jnp.float32),
            jax.ShapeDtypeStruct((batch, rows, D), jnp.bfloat16),
            row_shape,
            row_shape,
            row_shape,
        ],
        scratch_shapes=[pltpu.VMEM((rows, D), jnp.float32)],
        compiler_params=pltpu.CompilerParams(vmem_limit_bytes=56 * MEBI),
        cost_estimate=cost(
            flops=8 * batch * rows * D * D,
            bytes_accessed=batch * rows * D * 20 + 8 * D * D,
            transcendentals=0,
        ),
    )(*grads, *wholes, after_cross, scale_rows, cotangent)


def attend_input_kernel(
    g_ref, w_ref, x_ref, scale_ref, r_ref,
    gx_ref, shift_sum_ref, scale_sum_ref, g_sum_ref, acc_scr,
):
    step = pl.program_id(1)
    g_sum_ref[0] = jnp.sum(g_ref[0].astype(jnp.float32), axis=0, keepdims=True)

    @pl.when(step == 0)
    def _():
        acc_scr[...] = contract_last(g_ref[0], w_ref[...])

    @pl.when(step == 1)
    def _():
        acc_scr[...] += contract_last(g_ref[0], w_ref[...])

    @pl.when(step == 2)
    def _():
        sums = [0.0, 0.0]

        def product(part):
            return acc_scr[part] + contract_last(g_ref[0, part], w_ref[...])

        def use(part, grad):
            inputs = x_ref[0, part].astype(jnp.float32)
            inner, grad_shift, grad_scale = norm_backward(inputs, grad, scale_ref[0])
            gx_ref[0, part] = inner + r_ref[0, part]
            sums[0] += grad_shift
            sums[1] += grad_scale

        lagged(g_ref.shape[1], product, use)
        shift_sum_ref[0], scale_sum_ref[0] = sums


def attend_input(grad_qkv, weight, tokens, scale_rows, grad_attn):
    batch, rows = tokens.shape[:2]
    full = pl.BlockSpec((1, rows, D), lambda b, k: (b, 0, 0))
    row = pl.BlockSpec((1, 1, D), lambda b, k: (b, 0, 0))
    row_shape = jax.ShapeDtypeStruct((batch, 1, D), jnp.float32)
    return pl.pallas_call(
        attend_input_kernel,
        grid=(batch, 3),
        in_specs=[
            pl.BlockSpec((1, rows, D), lambda b, k: (b, 0, k)),
            pl.BlockSpec((D, D), lambda b, k: (0, k)),
            full,
            row,
            full,
        ],
        out_specs=[full, row, row, pl.BlockSpec((1, 1, D), lambda b, k: (b, 0, k))],
        out_shape=[
            jax.ShapeDtypeStruct((batch, rows, D), jnp.float32),
            row_shape,
            row_shape,
            jax.ShapeDtypeStruct((batch, 1, 3 * D), jnp.float32),
        ],
        scratch_shapes=[pltpu.VMEM((rows, D), jnp.float32)],
        compiler_params=pltpu.CompilerParams(vmem_limit_bytes=56 * MEBI),
        cost_estimate=cost(
            flops=6 * batch * rows * D * D,
            bytes_accessed=batch * rows * D * 16 + 6 * D * D,
            transcendentals=0,
        ),
    )(grad_qkv, weight, tokens, scale_rows, grad_attn)


def self_output_kernel(
    m_ref, wo_ref, bo_ref, x_ref, gate_ref, wq_ref, bq_ref, proj_ref, sum_ref, low_ref, query_ref
):
    def product(part):
        proj = matmul(m_ref[0, part], wo_ref[...]) + bo_ref[...]
        proj_ref[0, part] = proj
        after_attn = x_ref[0, part].astype(jnp.float32) + gate_ref[0] * proj
        sum_ref[0, part] = after_attn
        low_ref[0, part] = low(after_attn)
        return low(after_attn)

    def use(part, value):
        query_ref[0, part] = low(matmul(value, wq_ref[...]) + bq_ref[...])

    lagged(m_ref.shape[1], product, use, 128)


def self_output(mixed, w_out, out_bias, tokens, gate, w_query, query_bias):
    batch, rows = mixed.shape[:2]
    block = min(256, rows)
    part = pl.BlockSpec((1, block, D), lambda b, i: (b, i, 0))
    whole = pl.BlockSpec((D, D), lambda b, i: (0, 0))
    row = pl.BlockSpec((1, D), lambda b, i: (0, 0))
    wide = jax.ShapeDtypeStruct((batch, rows, D), jnp.float32)
    narrow = jax.ShapeDtypeStruct((batch, rows, D), jnp.bfloat16)
    return pl.pallas_call(
        self_output_kernel,
        grid=(batch, rows // block),
        in_specs=[
            part,
            whole,
            row,
            part,
            pl.BlockSpec((1, 1, D), lambda b, i: (b, 0, 0)),
            whole,
            row,
        ],
        out_specs=[part] * 4,
        out_shape=[wide, wide, narrow, narrow],
        compiler_params=pltpu.CompilerParams(vmem_limit_bytes=44 * MEBI),
        cost_estimate=cost(
            flops=4 * batch * rows * D * D,
            bytes_accessed=batch * rows * D * 16 + 4 * D * D,
            transcendentals=0,
        ),
    )(mixed, w_out, out_bias, tokens, gate, w_query, query_bias)


def cross_output_kernel(m_ref, w_ref, b_ref, x_ref, shift_ref, scale_ref, sum_ref, h_ref):
    def product(part):
        return matmul(m_ref[0, part], w_ref[...])

    def use(part, value):
        after_cross = x_ref[0, part] + (value + b_ref[...])
        sum_ref[0, part] = after_cross
        h_ref[0, part] = low(modulated(after_cross, shift_ref[0], scale_ref[0]))

    lagged(m_ref.shape[1], product, use, 128)


def cross_output(mixed, weight, bias, after_attn, shift_rows, scale_rows):
    batch, rows = mixed.shape[:2]
    block = min(256, rows)
    part = pl.BlockSpec((1, block, D), lambda b, i: (b, i, 0))
    row = pl.BlockSpec((1, 1, D), lambda b, i: (b, 0, 0))
    return pl.pallas_call(
        cross_output_kernel,
        grid=(batch, rows // block),
        in_specs=[
            part,
            pl.BlockSpec((D, D), lambda b, i: (0, 0)),
            pl.BlockSpec((1, D), lambda b, i: (0, 0)),
            part,
            row,
            row,
        ],
        out_specs=[part, part],
        out_shape=[
            jax.ShapeDtypeStruct((batch, rows, D), jnp.float32),
            jax.ShapeDtypeStruct((batch, rows, D), jnp.bfloat16),
        ],
        compiler_params=pltpu.CompilerParams(vmem_limit_bytes=36 * MEBI),
        cost_estimate=cost(
            flops=2 * batch * rows * D * D,
            bytes_accessed=batch * rows * D * 12 + 2 * D * D,
            transcendentals=0,
        ),
    )(mixed, weight, bias, after_attn, shift_rows, scale_rows)


def chip_flip(count, bit):
    return [(chip, chip ^ bit) for chip in range(count)]


def chip_shift(count, steps):
    return [(chip, (chip + 4 * steps) % count) for chip in range(count)]


def pick(tensor, index, axis):
    return lax.dynamic_index_in_dim(tensor, index, axis, keepdims=False)


def stack_kernel(*refs):
    for at, ref in enumerate(refs[:-1]):
        refs[-1][at] = ref[...]


def column_pieces(shard):
    count = lax.axis_size("fsdp")
    blocks = [shard] + [
        lax.ppermute(shard, "fsdp", chip_shift(count, -step)) for step in range(1, count // 4)
    ]
    return pl.pallas_call(
        stack_kernel,
        out_shape=jax.ShapeDtypeStruct((len(blocks), *shard.shape), shard.dtype),
        compiler_params=pltpu.CompilerParams(vmem_limit_bytes=32 * MEBI),
    )(*blocks)


def near_pieces(column):
    count = lax.axis_size("fsdp")
    return [
        column,
        lax.ppermute(column, "fsdp", chip_flip(count, 2)),
        lax.ppermute(column, "fsdp", chip_flip(count, 1)),
    ]


def far_pieces(near, split):
    count = lax.axis_size("fsdp")
    return [
        lax.ppermute(near[1][..., :split], "fsdp", chip_flip(count, 1)),
        lax.ppermute(near[2][..., split:], "fsdp", chip_flip(count, 2)),
    ]


def piece_columns(refs, start, width):
    blocks = []
    for ref in refs:
        columns = ref.shape[2]
        first, last = max(start, 0), min(start + width, columns)
        if first < last:
            blocks.append(ref[0, :, first:last])
        start -= columns
    return blocks


def assemble_kernel(regions, counts, place, *refs):
    y, x, core = place[1], place[2], place[3]
    sides = []
    for count in counts:
        sides.append(refs[:count])
        refs = refs[count:]

    def write(order):
        for flip_y, flip_x in ((0, 0), (1, 0), (0, 1), (1, 1)):
            chip = (y ^ flip_y) * 2 + (x ^ flip_x)
            near = flip_y + 2 * flip_x
            for out, (start, width) in zip(refs, regions):
                blocks = []
                for side in order:
                    pieces = sides[side][near : near + 1] if near < 3 else sides[side][3:]
                    blocks.extend(piece_columns(pieces, start, width))
                out[0, chip] = blocks[0] if len(blocks) == 1 else jnp.concatenate(blocks, axis=1)

    if len(counts) == 1:
        write((0,))
    else:
        pl.when(core == 0)(lambda: write((0, 1)))
        pl.when(core != 0)(lambda: write((1, 0)))


def assemble(sides, regions):
    count = lax.axis_size("fsdp")
    deep = count // 4
    chip = lax.axis_index("fsdp")
    place = jnp.stack([chip // 4, chip // 2 % 2, chip % 2, lax.axis_index("seq")])
    rows = sides[0][0].shape[1]
    widths = [len(sides) * width for _, width in regions]

    def from_z(i, place):
        return (lax.rem(i - place[0] + deep, deep), 0, 0)

    ins = [piece for side in sides for piece in side]
    outs = pl.pallas_call(
        functools.partial(assemble_kernel, regions, [len(side) for side in sides]),
        grid_spec=pltpu.PrefetchScalarGridSpec(
            num_scalar_prefetch=1,
            grid=(deep,),
            in_specs=[pl.BlockSpec((1, *piece.shape[1:]), from_z) for piece in ins],
            out_specs=[
                pl.BlockSpec((1, 4, rows, width), lambda i, place: (i, 0, 0, 0))
                for width in widths
            ],
        ),
        out_shape=[
            jax.ShapeDtypeStruct((deep, 4, rows, width), jnp.bfloat16) for width in widths
        ],
        compiler_params=pltpu.CompilerParams(vmem_limit_bytes=48 * MEBI),
        cost_estimate=cost(
            flops=0, bytes_accessed=16 * deep * rows * sum(widths), transcendentals=0
        ),
    )(place.astype(jnp.int32), *ins)
    return [out.reshape(count * rows, out.shape[-1]) for out in outs]


def gather_small(shard):
    count = lax.axis_size("fsdp")
    deep = count // 4
    z, y, x = chip_place()
    both = jnp.stack([shard, lax.ppermute(shard, "fsdp", chip_flip(count, 2))])
    both = jnp.where(y == 0, both, both[::-1])
    four = jnp.stack([both, lax.ppermute(both, "fsdp", chip_flip(count, 1))], axis=1)
    four = jnp.where(x == 0, four, four[:, ::-1])
    blocks = [four] + [
        lax.ppermute(four, "fsdp", chip_shift(count, -step)) for step in range(1, deep)
    ]
    blocks = jnp.stack(blocks + blocks[:-1])
    blocks = lax.dynamic_slice_in_dim(blocks, lax.rem(deep - z, deep), deep, 0)
    return blocks.reshape(count * shard.shape[0], shard.shape[1])


def chip_place():
    chip = lax.axis_index("fsdp")
    return chip // 4, chip // 2 % 2, chip % 2


def picks(blocks, index, axis):
    return jnp.concatenate([pick(block, index, axis) for block in blocks], axis=-1)


def sum_first(terms, x_first):
    count = lax.axis_size("fsdp")
    _, y, x = chip_place()
    blocks = [
        term.reshape(count // 4, 2, 2, term.shape[0] // count, term.shape[1]) for term in terms
    ]
    return blocks, picks(blocks, 1 - x, 2) if x_first else picks(blocks, 1 - y, 1)


def across_chips(kept, gone, bit, earlier):
    came = lax.ppermute(gone, "fsdp", chip_flip(lax.axis_size("fsdp"), bit))
    return low(kept.astype(jnp.float32) + after(came, earlier).astype(jnp.float32))


def sum_second(blocks, gone, x_first, earlier):
    _, y, x = chip_place()
    kept = picks(blocks, x, 2) if x_first else picks(blocks, y, 1)
    sums = across_chips(kept, gone, 1 if x_first else 2, earlier)
    return sums, pick(sums, 1 - y if x_first else 1 - x, 1)


def sum_third(sums, gone, x_first, earlier):
    _, y, x = chip_place()
    return across_chips(pick(sums, y if x_first else x, 1), gone, 2 if x_first else 1, earlier)


def along_z(*columns):
    column = jnp.concatenate(columns, axis=-1)
    deep, z = column.shape[0], chip_place()[0]
    return column, [pick(column, lax.rem(z + step, deep), 0) for step in range(1, deep)]


def sum_last(column, gones, earlier):
    count = lax.axis_size("fsdp")
    total = pick(column, chip_place()[0], 0).astype(jnp.float32)
    for step, gone in enumerate(gones, 1):
        came = lax.ppermute(gone, "fsdp", chip_shift(count, step))
        total += after(came, earlier).astype(jnp.float32)
    return total


def tie(*values):
    return lax.optimization_barrier(values)


def after(value, earlier):
    return lax.optimization_barrier((value, earlier))[0]


def column_sum(rows):
    return jnp.sum(rows.astype(jnp.float32), axis=0, keepdims=True)


def body(
    tokens, timestep, text, cotangent, vectors, w_qkv, w_out, w_query2, w_kv2, w_out2, w_fc1, w_fc2
):
    cores = lax.axis_size("seq")
    images = tokens.shape[0]
    swap = cores == 2 and images == 2
    core = lax.axis_index("seq")
    other = 1 - core
    across = [(0, 1), (1, 0)]
    rows_here = w_fc1.shape[0]

    def trade(rows):
        mine = lax.dynamic_slice_in_dim(rows, core, 1, 0)
        gone = lax.dynamic_slice_in_dim(rows, other, 1, 0)
        return jnp.concatenate([mine, lax.ppermute(gone, "seq", across)], axis=1)

    def trade_back(rows):
        half = rows.shape[1] // 2
        return by_core(rows[:, :half], pair(rows[:, half:]), 0)

    def by_core(mine, came, axis):
        return jnp.where(
            core == 0,
            jnp.concatenate([mine, came], axis=axis),
            jnp.concatenate([came, mine], axis=axis),
        )

    def pair(part):
        return lax.ppermute(part, "seq", across)

    def mlp_shard():
        here = w_fc1.reshape(rows_here, -1, 2, 2, rows_here)
        gone, mine = pick(here, other, 2), pick(here, core, 2)
        first = by_core(mine, pair(gone), 1)
        first = first.transpose(0, 2, 1, 3).reshape(rows_here, -1)
        here = w_fc2.reshape(2, 2, rows_here, -1)
        gone, mine = pick(here, other, 0), pick(here, core, 0)
        second = by_core(mine, pair(gone), 2)
        return jnp.concatenate([first, second[0], second[1]], axis=1)

    def whole_rest(near, earlier):
        near = after(near, earlier)
        pieces = [*near, *far_pieces(near, 1408)]
        half = w_out.shape[1]
        return assemble(
            [pieces, [pair(piece) for piece in pieces]],
            [(0, half), (half, half), (2 * half, 2 * half), (4 * half, half)],
        )

    def gather_plain():
        whole = [
            lax.all_gather(
                lax.all_gather(part, "fsdp", axis=0, tiled=True), "seq", axis=1, tiled=True
            )
            for part in (w_qkv, w_out, w_query2, w_kv2, w_out2, w_fc1, w_fc2)
        ]
        first, second = whole[5:]
        mlp = [
            jnp.concatenate(
                [
                    first[:, 2 * part * D : 2 * (part + 1) * D],
                    second[2 * part * D : (2 * part + 1) * D],
                    second[(2 * part + 1) * D : 2 * (part + 1) * D],
                ],
                axis=1,
            )
            for part in range(2)
        ]
        return (*whole[:5], mlp)

    def core_parts(right):
        width = (right.shape[1] // 2 + 127) // 128 * 128
        low_part, high_part = right[:, :width], right[:, -width:]
        return (
            jnp.where(core == 0, high_part, low_part),
            jnp.where(core == 0, low_part, high_part),
        )

    def pair_send(left, right):
        return low(dot_tn(left, core_parts(right)[0]))

    def pair_sum(left, right, sent):
        return low(dot_tn(left, core_parts(right)[1]) + pair(sent).astype(jnp.float32))

    def pair_grad(left, right):
        return pair_sum(left, right, pair_send(left, right))

    def own_half(wide, place):
        return jnp.where(place == 0, wide[:, :-64], wide[:, 64:])

    def weight_grad(left, right):
        return scatter_plain(low(dot_tn(left, right)))

    def scatter_plain(full):
        part = lax.psum_scatter(full, "seq", scatter_dimension=1, tiled=True)
        return lax.psum_scatter(part, "fsdp", scatter_dimension=0, tiled=True).astype(jnp.float32)

    if swap:
        shard, vectors, tokens, text, cotangent = tie(
            mlp_shard(), vectors, tokens, text, cotangent
        )
        mlp_own = lax.all_gather(shard, "fsdp", axis=0, tiled=True)
        column = column_pieces(w_qkv)
        vec = gather_small(jnp.pad(vectors, ((0, 0), (0, 128 - vectors.shape[1]))))
        tokens, text, cotangent = trade(tokens), trade(text), trade(cotangent)
        column, vec, tokens, text, cotangent, others = tie(
            column, vec, tokens, text, cotangent, (w_out, w_query2, w_kv2, w_out2)
        )
        near = near_pieces(column)
        rest = column_pieces(jnp.concatenate(others, axis=1))
        far, rest = tie(far_pieces(near, 896), rest)
        rest_near = near_pieces(rest)
        pieces = [*near, *far]
        (wf_qkv,) = assemble([pieces, [pair(piece) for piece in pieces]], [(0, w_qkv.shape[1])])
        vec = vec.T[: vectors.shape[1]].astype(jnp.float32)
        timestep = lax.dynamic_slice_in_dim(timestep, core, 1, 0)
    batch, rows = tokens.shape[0], tokens.shape[1]
    if not swap:
        vec = lax.all_gather(vectors, "fsdp", axis=0, tiled=True).T.astype(jnp.float32)
        wf_qkv, wf_out, wf_query2, wf_kv2, wf_out2, mlp = gather_plain()

    def unflat(tensor):
        return tensor.reshape(batch, rows, tensor.shape[-1])

    inputs = tokens.astype(jnp.float32)
    modulation = vec[None, :6] + timestep.astype(jnp.float32).reshape(batch, 6, D)
    zero_bias = jnp.zeros((1, D), jnp.float32)
    h_attn = lax.optimization_barrier(
        low(modulated(inputs, modulation[:, 0:1], modulation[:, 1:2]))
    )
    qkv_bias = jnp.concatenate([vec[6:7], zero_bias, vec[7:8]], axis=1)
    qkv_rows = unflat(low(matmul(flatten(h_attn), wf_qkv) + qkv_bias))
    if swap:
        self_qkv = ((qkv_rows, 0), (qkv_rows, 1), (qkv_rows, 2))
    else:
        all_kv = lax.all_gather(qkv_rows[..., D:], "seq", axis=1, tiled=True)
        self_qkv = ((qkv_rows, 0), (all_kv, 0), (all_kv, 1))
    attn_low, self_lse = attend_forward(*self_qkv, 512)
    if swap:
        wf_out, wf_query2, wf_kv2, wf_out2 = whole_rest(rest_near, attn_low)
    attn_proj, after_attn, after_low, cross_query = self_output(
        attn_low, wf_out, vec[8:9], tokens, modulation[:, 2:3], wf_query2, vec[9:10]
    )
    kv_bias = jnp.concatenate([zero_bias, vec[10:11]], axis=1)
    text_kv = low(matmul(flatten(text), wf_kv2) + kv_bias).reshape(batch, text.shape[1], 2 * D)
    if not swap:
        text_kv = lax.all_gather(text_kv, "seq", axis=1, tiled=True)
    cross_qkv = ((cross_query, 0), (text_kv, 0), (text_kv, 1))
    cross_low, cross_lse = attend_forward(*cross_qkv, 1024)
    after_cross, h_mlp = cross_output(
        cross_low, wf_out2, vec[11:12], after_attn, modulation[:, 3:4], modulation[:, 4:5]
    )
    fc1_bias = vec[13:].reshape(1, -1)
    if swap:
        fc1_bias = fc1_bias.reshape(-1, 2, 2, rows_here)
        biases = [
            pick(fc1_bias, place, 1).transpose(1, 0, 2).reshape(1, -1) for place in (core, other)
        ]
    else:
        biases = [fc1_bias[:, : 2 * D], fc1_bias[:, 2 * D :]]
    if swap:
        mlp = (mlp_own, pair(after(mlp_own, h_mlp)))
    hidden = [mlp_first(h_mlp, whole, bias) for whole, bias in zip(mlp, biases)]
    lows = [hidden_low for hidden_low, _ in hidden]
    result, grad_mlp, grad_gate_mlp, fc2_sums = mlp_second(
        lows, mlp, vec[12:13], after_cross, modulation[:, 5:6], cotangent
    )

    def small_sums():
        grad_time = jnp.concatenate(
            [
                grad_shift_attn,
                grad_scale_attn,
                grad_gate_attn,
                grad_shift_mlp,
                grad_scale_mlp,
                grad_gate_mlp,
            ],
            axis=1,
        )
        qkv_rows_sum = jnp.sum(qkv_sums, axis=0)
        grad_vectors = jnp.concatenate(
            [
                jnp.sum(grad_time, axis=0),
                qkv_rows_sum[:, :D],
                qkv_rows_sum[:, 2 * D :],
                *small[1:],
                jnp.sum(out2_sums, axis=0),
                jnp.sum(fc2_sums, axis=0),
                fc1_sums.reshape(-1, D),
            ],
            axis=0,
        ).T
        return grad_time, grad_vectors

    flat_h, flat_gm = flatten(h_mlp), flatten(grad_mlp)
    if swap:
        own_low, other_low = flatten(lows[0]), flatten(lows[1])
        sent = low(dot_tn(other_low, flat_gm))
        sent, grad_mlp = tie(sent, grad_mlp)
        other_pre, other_sums = mlp_slope(grad_mlp, mlp[1], hidden[1][1])
        fc2_part = low(dot_tn(own_low, flat_gm) + pair(sent).astype(jnp.float32))
        fc2_x, fc2_gone_x = sum_first([fc2_part[:D]], True)
        fc2_y, fc2_gone_y = sum_first([fc2_part[D:]], False)
        fc2_gone_x, fc2_gone_y, other_pre, grad_mlp = tie(
            fc2_gone_x, fc2_gone_y, other_pre, grad_mlp
        )
        sent = low(dot_tn(flat_h, flatten(other_pre)))
        sent, grad_mlp = tie(sent, grad_mlp)
        own_pre, own_sums = mlp_slope(grad_mlp, mlp[0], hidden[0][1])
        fc1_part = low(dot_tn(flat_h, flatten(own_pre)) + pair(sent).astype(jnp.float32))
        fc1_x, fc1_gone_x = sum_first([fc1_part[:, :D]], True)
        fc1_y, fc1_gone_y = sum_first([fc1_part[:, D:]], False)
        fc2_x, fc2_gone_x = sum_second(fc2_x, fc2_gone_x, True, fc1_gone_x)
        fc2_y, fc2_gone_y = sum_second(fc2_y, fc2_gone_y, False, fc1_gone_y)
        own_pre, fc1_gone_x, fc1_gone_y, fc2_gone_x, fc2_gone_y = tie(
            own_pre, fc1_gone_x, fc1_gone_y, fc2_gone_x, fc2_gone_y
        )
        result = after(result, fc1_gone_x)
        grads_pre, fc1_sums = [own_pre, other_pre], [own_sums, other_sums]
    else:
        slopes = [mlp_slope(grad_mlp, whole, slope) for whole, (_, slope) in zip(mlp, hidden)]
        grads_pre = [grad_pre for grad_pre, _ in slopes]
        fc1_sums = [sums for _, sums in slopes]
    fc1_sums = [jnp.sum(sums, axis=0) for sums in fc1_sums]
    if swap:
        fc1_sums = by_core(fc1_sums[0], fc1_sums[1], 1).reshape(2, 2, -1, rows_here)
        fc1_sums = fc1_sums.transpose(2, 0, 1, 3)
    grad_cross, grad_proj2, grad_shift_mlp, grad_scale_mlp, out2_sums = mlp_input(
        grads_pre, mlp, after_cross, modulation[:, 4:5], cotangent
    )
    grad_proj2 = flatten(grad_proj2)
    if swap:
        fc1_x, fc1_gone_x = sum_second(fc1_x, fc1_gone_x, True, grad_proj2)
        fc1_y, fc1_gone_y = sum_second(fc1_y, fc1_gone_y, False, grad_proj2)
        fc1_gone_x, fc1_gone_y, grad_proj2 = tie(fc1_gone_x, fc1_gone_y, grad_proj2)
    grad_mixed2 = unflat(low(dot_nt(grad_proj2, wf_out2)))
    if swap:
        out2_part = pair_grad(flatten(cross_low), grad_proj2)
        grad_mixed2, out2_part = tie(grad_mixed2, out2_part)
    grad_q2, grad_kv = attend_backward(
        *cross_qkv, grad_mixed2, cross_low, cross_lse, 1024, False,
        jnp.bfloat16 if swap else jnp.float32,
    )
    if not swap:
        grad_kv = low(lax.psum_scatter(grad_kv, "seq", scatter_dimension=1, tiled=True))
    grad_kv, grad_q2 = flatten(grad_kv), flatten(grad_q2)
    if swap:
        mlp_column, mlp_gones = along_z(
            sum_third(fc1_x, fc1_gone_x, True, grad_q2),
            sum_third(fc1_y, fc1_gone_y, False, grad_q2),
            sum_third(fc2_x, fc2_gone_x, True, grad_q2),
            sum_third(fc2_y, fc2_gone_y, False, grad_q2),
        )
        mlp_gones, grad_q2, grad_kv = tie(mlp_gones, grad_q2, grad_kv)
    grad_text = dot_nt(grad_kv, wf_kv2).reshape(text.shape)
    grad_attn = grad_cross + unflat(dot_nt(grad_q2, wf_query2))
    grad_gate_attn = jnp.sum(grad_attn * attn_proj, axis=1, keepdims=True)
    grad_proj1 = flatten(low(modulation[:, 2:3] * grad_attn))
    grad_mixed1 = unflat(low(dot_nt(grad_proj1, wf_out)))
    if swap:
        rest_x, gone_x = sum_first(
            [
                pair_grad(flatten(text), grad_kv),
                pair_grad(flatten(attn_low), grad_proj1),
            ],
            True,
        )
        rest_y, gone_y = sum_first(
            [out2_part, pair_grad(flatten(after_low), grad_q2)], False
        )
        small = (grad_text, column_sum(grad_proj1), column_sum(grad_q2), column_sum(grad_kv[:, D:]))
        gone_x, gone_y, grad_mixed1, small = tie(gone_x, gone_y, grad_mixed1, small)
        grad_text = small[0]
        (grad_qkv_low,) = attend_backward(
            *self_qkv, grad_mixed1, attn_low, self_lse, 256, True, jnp.bfloat16
        )
        grad_qkv_low = flatten(grad_qkv_low)
        rest_x, gone_x = sum_second(rest_x, gone_x, True, grad_qkv_low)
        rest_y, gone_y = sum_second(rest_y, gone_y, False, grad_qkv_low)
        mlp_part = sum_last(mlp_column, mlp_gones, grad_qkv_low)
        gone_x, gone_y, mlp_part, grad_qkv_low = tie(gone_x, gone_y, mlp_part, grad_qkv_low)
        qkv_part = pair_grad(flatten(h_attn), grad_qkv_low)
        columns = qkv_part.shape[1] // 2
        qkv_x, qkv_gone_x = sum_first([qkv_part[:, :columns]], True)
        qkv_y, qkv_gone_y = sum_first([qkv_part[:, columns:]], False)
        column, gones = along_z(
            sum_third(rest_x, gone_x, True, qkv_gone_x),
            sum_third(rest_y, gone_y, False, qkv_gone_y),
        )
        gones, qkv_gone_x, qkv_gone_y, grad_qkv_low = tie(
            gones, qkv_gone_x, qkv_gone_y, grad_qkv_low
        )
        grad_tokens, grad_shift_attn, grad_scale_attn, qkv_sums = attend_input(
            unflat(grad_qkv_low), wf_qkv, tokens, modulation[:, 1:2], grad_attn
        )
        qkv_x, gone_x = sum_second(qkv_x, qkv_gone_x, True, grad_shift_attn)
        qkv_y, gone_y = sum_second(qkv_y, qkv_gone_y, False, grad_shift_attn)
        gone_x, gone_y, grad_tokens, grad_shift_attn, grad_scale_attn, qkv_sums = tie(
            gone_x, gone_y, grad_tokens, grad_shift_attn, grad_scale_attn, qkv_sums
        )
        rest = sum_last(column, gones, gone_x)
        grad_time, grad_vectors = small_sums()
        count = grad_vectors.shape[1]
        part = low(jnp.pad(grad_vectors, ((0, 0), (0, 128 - count))))
        part = low(part.astype(jnp.float32) + pair(part).astype(jnp.float32))
        blocks, gone = sum_first([part], True)
        sums, gone = sum_second(blocks, gone, True, part)
        grad_tokens = trade_back(grad_tokens)
        column, gones = along_z(
            sum_third(qkv_x, gone_x, True, grad_tokens),
            sum_third(qkv_y, gone_y, False, grad_tokens),
        )
        grad_qkv = own_half(sum_last(column, gones, rest), core)
        vec_column, vec_gones = along_z(sum_third(sums, gone, True, gones[0]))
        grad_vectors = sum_last(vec_column, vec_gones, rest)[:, :count]
        mlp_part, grad_text = after((mlp_part, grad_text), gones[0])
        grad_kv2 = rest[:, : 2 * w_out.shape[1]]
        grad_out, grad_out2, grad_query2 = [
            own_half(part, core) for part in jnp.split(rest[:, grad_kv2.shape[1] :], 3, axis=1)
        ]
        here = mlp_part[:, : 2 * D].reshape(rows_here, 2, -1, rows_here).transpose(0, 2, 1, 3)
        here = here.reshape(rows_here, 2, -1, 2, rows_here)
        gone, mine = pick(here, other, 1), pick(here, core, 1)
        grad_fc1 = by_core(mine[:, :, None], pair(gone)[:, :, None], 2).reshape(w_fc1.shape)
        here = jnp.concatenate([mlp_part[:, 2 * D : 3 * D], mlp_part[:, 3 * D :]], axis=0)
        gone, mine = core_parts(here)
        gone, mine = own_half(gone, other), own_half(mine, core)
        grad_fc2 = by_core(mine, pair(gone), 0)
    else:
        grad_q, grad_kv1 = attend_backward(
            *self_qkv, grad_mixed1, attn_low, self_lse, 256, False, jnp.float32
        )
        grad_kv1 = lax.psum_scatter(grad_kv1, "seq", scatter_dimension=1, tiled=True)
        grad_qkv_low = flatten(jnp.concatenate([grad_q, low(grad_kv1)], axis=-1))
        grad_tokens, grad_shift_attn, grad_scale_attn, qkv_sums = attend_input(
            unflat(grad_qkv_low), wf_qkv, tokens, modulation[:, 1:2], grad_attn
        )
        grad_fc1 = scatter_plain(
            jnp.concatenate([low(dot_tn(flat_h, flatten(part))) for part in grads_pre], axis=1)
        )
        grad_fc2 = scatter_plain(
            jnp.concatenate([low(dot_tn(flatten(part), flat_gm)) for part in lows], axis=0)
        )
        grad_out2 = weight_grad(flatten(cross_low), grad_proj2)
        grad_kv2 = weight_grad(flatten(text), grad_kv)
        grad_query2 = weight_grad(flatten(after_low), grad_q2)
        grad_out = weight_grad(flatten(attn_low), grad_proj1)
        grad_qkv = weight_grad(flatten(h_attn), grad_qkv_low)
        fc1_sums = jnp.concatenate(fc1_sums, axis=1)
        small = (grad_text, column_sum(grad_proj1), column_sum(grad_q2), column_sum(grad_kv[:, D:]))
        grad_time, grad_vectors = small_sums()
        grad_vectors = lax.psum_scatter(
            lax.psum(grad_vectors, "seq"), "fsdp", scatter_dimension=0, tiled=True
        )
    grad_time = grad_time.reshape(batch, 6 * D)
    if swap:
        grad_time = by_core(grad_time, pair(grad_time), 0)
        result, grad_text = trade_back(result), trade_back(grad_text)
    else:
        grad_time = lax.psum(grad_time, "seq")
    return (
        result,
        grad_tokens,
        grad_time,
        grad_text,
        grad_vectors,
        grad_qkv,
        grad_out,
        grad_query2,
        grad_kv2,
        grad_out2,
        grad_fc1,
        grad_fc2,
    )


def solution(mesh):
    in_specs = (
        P("fsdp", "seq", None),
        P("fsdp", None),
        P("fsdp", "seq", None),
        P("fsdp", "seq", None),
        P("fsdp", None),
        P("fsdp", "seq"),
        P("fsdp", "seq"),
        P("fsdp", "seq"),
        P("fsdp", "seq"),
        P("fsdp", "seq"),
        P("fsdp", "seq"),
        P("fsdp", "seq"),
    )
    out_specs = (
        P("fsdp", "seq", None),
        P("fsdp", "seq", None),
        P("fsdp", None),
        P("fsdp", "seq", None),
        P("fsdp", None),
        P("fsdp", "seq"),
        P("fsdp", "seq"),
        P("fsdp", "seq"),
        P("fsdp", "seq"),
        P("fsdp", "seq"),
        P("fsdp", "seq"),
        P("fsdp", "seq"),
    )
    return jax.shard_map(body, mesh=mesh, in_specs=in_specs, out_specs=out_specs, check_vma=False)
```
